32 devices in a mesh: row: 2 (over y), col: 16 (over z, x, core).
Axes of the slice: x: 2, y: 2, z: 4, core: 2. Of those that a mesh axis runs over, the one named last changes fastest.
Arguments:
- transfer: bfloat16 [2, 512, 16384], P(None, 'row', 'col'), may hold values from -0.046875 to 0.046875
- phase: float32 [16384, 128], P('col', 'row'), may hold values from -3.140625 to 3.140625
- trap_index: int32 [128, 64], replicated, may hold values from 0 to 511
- levels: int32 [128, 64], replicated, may hold values from 1 to 4
- weights_old: float32 [128, 64], replicated, may hold values from 0.5 to 1.5
Outputs:
- far_field: bfloat16 [512, 2, 128], P(('row', 'col'))
- weights_new: float32 [128, 64], replicated
- slm_field: float32 [16384, 2, 128], P('col', None, 'row')
The draws below stay inside these ranges and needn't reach their ends.
All inputs are finite; a program needn't handle non-finite values.
Results may differ from the reference program's by a relative error of at most 0.013.
Values may be sent and summed in bfloat16 or wider, within the bound.
No kernel may reach another device: no remote copies, remote signals or barrier semaphores. Data moves between devices by JAX's collectives and lax.ppermute only.
A program may use at most 64 MiB of HBM per device.

```python
import jax
import jax.numpy as jnp
from jax import lax

MODES = 16384
PATTERNS = 128
TRAPS = 64
M = 512


def place_ends(array, stream_key, smallest, top_value):
    shape = array.shape
    spot = [jax.random.randint(jax.random.fold_in(stream_key, axis), (), 0, shape[axis]) for axis in range(len(shape))]
    array = array.at[tuple(spot)].set(smallest)
    longest = shape.index(max(shape))
    spot[longest] = (spot[longest] + 1) % shape[longest]
    return array.at[tuple(spot)].set(top_value)


def level_of(stream_key, shape, pieces, least, high):
    level = 1.0
    for position, blocks in pieces:
        steps = jax.random.uniform(jax.random.fold_in(jax.random.fold_in(stream_key, 6), position), (blocks,), jnp.float32, least / len(pieces), high / len(pieces))
        level = level * jnp.repeat(jnp.exp(steps), shape[position] // blocks).reshape((-1,) + (1,) * (len(shape) - 1 - position))
    return level


def scatter_about(own_key, extent, width, limit, split=(), kind=jnp.bfloat16):
    drawn = width * jax.random.normal(own_key, extent, jnp.float32)
    if split:
        drawn = drawn * level_of(own_key, extent, split, -0.22, 0.18)
    return jnp.clip(drawn, -limit, limit).astype(kind)


def setup_inputs(seed: int = 0) -> dict:
    key_of = jax.random.split(jax.random.key(seed), 6)
    transfer = scatter_about(key_of[0], (2, M, MODES), MODES ** -0.5, 0.046875, ((1, 2), (2, 16)))
    phase = jnp.clip(jax.random.uniform(key_of[1], (MODES, PATTERNS), jnp.float32, -3.140625, 3.140625), -3.140625, 3.140625)
    trap_index = place_ends(jax.random.randint(key_of[2], (PATTERNS, TRAPS), 0, M), jax.random.fold_in(key_of[2], 1), 0, M - 1).astype(jnp.int32)
    levels = place_ends(jax.random.randint(key_of[3], (PATTERNS, TRAPS), 1, 5), jax.random.fold_in(key_of[3], 1), 1, 4).astype(jnp.int32)
    weights_old = jnp.clip(1.0 + 0.1 * jax.random.normal(key_of[4], (PATTERNS, TRAPS), jnp.float32), 0.5, 1.5)
    return {"transfer": transfer, "phase": phase, "trap_index": trap_index, "levels": levels, "weights_old": weights_old}


def reference(transfer, phase, trap_index, levels, weights_old):
    count = phase.shape[1]
    field_re = jnp.cos(phase).astype(jnp.bfloat16)
    field_im = jnp.sin(phase).astype(jnp.bfloat16)
    joined = jnp.concatenate([field_re, field_im], axis=1)
    first = jnp.dot(transfer[0], joined, preferred_element_type=jnp.float32)
    second = jnp.dot(transfer[1], joined, preferred_element_type=jnp.float32)
    out = jnp.stack([first[:, :count] - second[:, count:], first[:, count:] + second[:, :count]], axis=1)
    far_field = out.astype(jnp.bfloat16)
    pattern_ids = jnp.arange(count, dtype=jnp.int32)[:, None]
    values = out[trap_index, :, pattern_ids]
    amp = jnp.sqrt(values[..., 0] ** 2 + values[..., 1] ** 2 + 0.25)
    target = levels.astype(jnp.float32)
    ratio = amp / target
    mean_ratio = lax.optimization_barrier(jnp.mean(ratio, axis=1, keepdims=True))
    weights_new = weights_old * mean_ratio / ratio
    coef = weights_new * target / amp
    projected = jnp.zeros(out.shape, jnp.float32).at[trap_index, :, pattern_ids].add(coef[..., None] * values)
    projected = projected.astype(jnp.bfloat16)
    stacked = jnp.concatenate([projected[:, 0], projected[:, 1]], axis=1)
    dims = (((0,), (0,)), ((), ()))
    first_b = lax.dot_general(transfer[0], stacked, dims, preferred_element_type=jnp.float32)
    second_b = lax.dot_general(transfer[1], stacked, dims, preferred_element_type=jnp.float32)
    back = jnp.stack([first_b[:, :count] + second_b[:, count:], first_b[:, count:] - second_b[:, :count]], axis=1)
    scaled = jnp.sqrt(jnp.float32(MODES) / jnp.float32(TRAPS)) * back
    slm_field = scaled / jnp.sqrt(scaled[:, 0:1] ** 2 + scaled[:, 1:2] ** 2 + 1.0)
    return (far_field, weights_new, slm_field)
```

```python
import functools

import jax
import jax.numpy as jnp
from jax import lax
from jax.experimental import pallas as pl
from jax.experimental.pallas import tpu as pltpu
from jax.sharding import PartitionSpec as P

MODES = 16384
TRAPS = 64
BF = jnp.bfloat16
F32 = jnp.float32
AXES = ("row", "col")
LANES = 128
SIN = (0.9999996052826214, -0.16666553769418907, 0.008332409691364227, -0.00019808794770261517, 2.6998844729663915e-06,
       -2.0368733379709898e-08)
COS = (0.999999989217114, -0.49999989221470714, 0.041666490704389186, -0.0013887810304225767, 2.4770020037729276e-05,
       -2.708030902998698e-07, 1.7249574387300172e-09)
STEEP = 25.0
CROSS = ()
NT = (((1,), (1,)), ((), ()))
NN = (((1,), (0,)), ((), ()))
SMEM = pl.BlockSpec(memory_space=pltpu.SMEM)
VMEM = pl.BlockSpec(memory_space=pltpu.VMEM)


def call(kernel, name, outs, ins, out_specs=None, scratch=(), flops=0, size=0):
    return pl.pallas_call(
        kernel,
        out_shape=[jax.ShapeDtypeStruct(s, d) for s, d in outs],
        in_specs=ins,
        out_specs=out_specs or [VMEM] * len(outs),
        scratch_shapes=list(scratch),
        compiler_params=pltpu.CompilerParams(vmem_limit_bytes=40 * 1024 * 1024),
        cost_estimate=pl.CostEstimate(flops=flops, bytes_accessed=size, transcendentals=0),
        name=name,
    )


def bits_of(n):
    return n.bit_length() - 1


def padded(n):
    return -(-2 * n // LANES) * LANES


def horner(coefs, y):
    acc = jnp.full_like(y, coefs[-1])
    for c in coefs[-2::-1]:
        acc = acc * y + c
    return acc


def swap_pairs(x, mask):
    n = lax.axis_size("row") * lax.axis_size("col")
    return lax.ppermute(x, AXES, [(i, i ^ mask) for i in range(n)])


def lane_of(x):
    return lax.broadcasted_iota(jnp.int32, x.shape, x.ndim - 1)


def turn(x, by):
    lanes = x.shape[-1]
    by = by % lanes
    return x if by == 0 else pltpu.roll(x, lanes - by, x.ndim - 1)


def flip_blocks(x, width, bit):
    w = width << bit
    return jnp.where((lane_of(x) // w) % 2 == 1, turn(x, -w), turn(x, w))


def spread(x, base, n):
    parts = []
    for c in range(padded(n) // LANES):
        at = LANES * c
        first, second = turn(x, at + base), turn(x, at + base - n)
        parts.append(jnp.where(lane_of(x) + at < n, first, second))
    return parts[0] if len(parts) == 1 else jnp.concatenate(parts, axis=1)


def partner(x, n):
    return jnp.where(lane_of(x) < n, turn(x, n), turn(x, -n))


def tree_sum(parts):
    while len(parts) > 1:
        parts = [parts[i] + parts[i + 1] for i in range(0, len(parts), 2)]
    return parts[0]


def relative(x, row, per_row):
    for b in range(bits_of(x.shape[1] // per_row)):
        x = jnp.where(((row >> b) & 1) == 1, flip_blocks(x, per_row, b), x)
    return x


def project(phase, t_ref, index, out_ref, ready=None):
    n = phase.shape[0]
    rows = t_ref.shape[1]
    traps, lanes = index.shape
    y = phase * phase
    co = horner(COS, y).astype(BF)
    si = (phase * horner(SIN, y)).astype(BF)
    fill = [jnp.zeros((lanes - 2 * n, phase.shape[1]), BF)] if lanes > 2 * n else []
    if ready is not None:
        ready.wait()
    out_ref[...] = lax.dot_general(
        t_ref[0], jnp.concatenate([co, si] + fill, axis=0), NT, preferred_element_type=F32
    ) + lax.dot_general(t_ref[1], jnp.concatenate([-si, co] + fill, axis=0), NT, preferred_element_type=F32)
    found = []
    for g in range(traps // 8):
        high = index[g * 8:(g + 1) * 8] >> 3
        low = index[g * 8:(g + 1) * 8] & 7
        got = jnp.zeros((8, lanes), F32)
        for h in range(rows // 8):
            got = jnp.where(high == h, jnp.take_along_axis(out_ref[h * 8:(h + 1) * 8, :], low, axis=0), got)
        found.append(got)
    return found


def own_kernel(place_ref, ph_ref, index_ref, transfer_ref, out_ref, trap_ref, t_ref, sem):
    bring = pltpu.make_async_copy(transfer_ref, t_ref, sem)
    bring.start()
    per_row = ph_ref.shape[0]
    row = place_ref[0]
    index = spread(relative(index_ref[...], row, per_row) - row * t_ref.shape[1], 0, per_row)
    for g, got in enumerate(project(ph_ref[...], t_ref, index, out_ref, bring)):
        trap_ref[g * 8:(g + 1) * 8, :] = got


def other_kernel(order, per_row, place_ref, code_ref, index_ref, t_ref, own_ref, own_trap_ref, keep_ref, send_ref, out_ref):
    row, col = place_ref[0], place_ref[1]
    traps, count = index_ref.shape
    rows = t_ref.shape[1]
    index = spread(relative(index_ref[...], row, per_row) - row * rows, per_row, count - per_row)
    code = code_ref[...].astype(F32)
    size = jnp.log(jnp.abs(code)) * (1.0 / STEEP)
    found = project(jnp.where(code < 0, -size, size), t_ref, index, out_ref)
    n_own = own_ref.shape[1] // LANES
    sets = [(own_ref, c) for c in range(n_own)] + [(out_ref, c) for c in range(out_ref.shape[1] // LANES)]
    parts = len(sets)
    n_send = send_ref.shape[0] - 2 * parts * traps
    for g in range(traps // 8):
        for p, (ref, c) in enumerate(sets):
            lanes = slice(c * LANES, (c + 1) * LANES)
            value = own_trap_ref[g * 8:(g + 1) * 8, lanes] if p < n_own else found[g][:, lanes]
            large = value.astype(BF)
            at = n_send + p * traps + g * 8
            send_ref[at:at + 8, :] = large
            at += parts * traps
            send_ref[at:at + 8, :] = (value - large.astype(F32)).astype(BF)
    px = rows // len(order)
    half = len(order) // 2
    for s, j in enumerate(order):
        start = pl.multiple_of((col ^ j) * px, px)
        for p, (ref, c) in enumerate(sets):
            piece = ref[pl.ds(start, px), c * LANES:(c + 1) * LANES]
            at = ((s % half) * parts + p) * px
            if s < half:
                keep_ref[at:at + px, :] = piece
            else:
                send_ref[at:at + px, :] = piece.astype(BF)


def plan_kernel(per_row, rows, cross, place_ref, index_ref, levels_ref, old_ref, *refs):
    row = place_ref[0]
    traps, count = index_ref.shape
    index = relative(index_ref[...], row, per_row)
    target = relative(levels_ref[...], row, per_row).astype(F32)
    old = relative(old_ref[...], row, per_row)
    refs[0][...] = old
    inverse = 1.0 / target
    numer = old * (target * target)
    now_ref = refs[-1]
    group = 4

    def slots(pixels, outs):
        now_ref[...] = pixels

        def find(g, carry):
            base = pl.multiple_of(g * (8 * group), 8 * group)
            pixel = lax.broadcasted_iota(jnp.int32, (8, count), 0) + base
            acc = [jnp.full((8, count), -1, jnp.int32) for _ in range(group)]
            for k in range(traps):
                ind = jnp.broadcast_to(now_ref[k:k + 1, :], (8, count))
                for i in range(group):
                    acc[i] = jnp.where(ind == pixel + 8 * i, k, acc[i])
            for i in range(group):
                for ref, base_lane, n in outs:
                    ref[pl.ds(base + 8 * i, 8), :] = spread(acc[i], base_lane, n)
            return carry

        lax.fori_loop(0, rows // (8 * group), find, 0)

    mine = index - row * rows
    sets = ((0, per_row), (per_row, count - per_row))
    for s, (base, n) in enumerate(sets):
        idx_ref, inv_ref, num_ref, _ = refs[1 + 4 * s:5 + 4 * s]
        idx_ref[...] = spread(mine, base, n)
        inv_ref[...] = spread(inverse, base, n)
        num_ref[...] = spread(numer, base, n)
    slots(mine, [(refs[4], *sets[0]), (refs[8], *sets[1])])
    if cross:
        theirs = index - (1 - row) * rows
        refs[9][...] = spread(theirs, *sets[0])
        slots(theirs, [(refs[10], *sets[0])])


def scatter(idx_ref, value_ref, slot_ref, px_ref, n):
    traps, lanes = idx_ref.shape
    index = idx_ref[...]
    acc = [jnp.zeros((8, lanes), F32) for _ in range(traps // 8)]
    for k in range(traps):
        ind = jnp.broadcast_to(idx_ref[k:k + 1, :], (8, lanes))
        val = jnp.broadcast_to(value_ref[k:k + 1, :], (8, lanes))
        for g in range(traps // 8):
            acc[g] += jnp.where(index[g * 8:(g + 1) * 8, :] == ind, val, 0.0)
    for h in range(slot_ref.shape[0] // 8):
        slot = slot_ref[h * 8:(h + 1) * 8, :]
        high = slot >> 3
        low = slot & 7
        got = jnp.zeros((8, lanes), F32)
        for g in range(traps // 8):
            got = jnp.where(high == g, jnp.take_along_axis(acc[g], low, axis=0), got)
        px_ref[h * 8:(h + 1) * 8, :] = got
    proj = px_ref[...].T.astype(BF)
    turned = [proj[n:2 * n], -proj[:n]] + ([proj[2 * n:]] if lanes > 2 * n else [])
    return proj, jnp.concatenate(turned, axis=0)


def back_through(pair, t_ref, modes):
    return lax.dot_general(pair[0], t_ref[0, :, modes], NN, preferred_element_type=F32) + lax.dot_general(
        pair[1], t_ref[1, :, modes], NN, preferred_element_type=F32
    )


def values_kernel(per_row, crossing, own_ref, got_ref, t_ref, *refs):
    sets = (refs[0:3], refs[3:6])
    slot_ref, value_own_ref, away_ref, value_oth_ref, px_ref = refs[6:]
    rows, modes = t_ref.shape[1:]
    traps = sets[0][0].shape[0]
    ratios = []
    part = 0
    for (idx_ref, inv_ref, num_ref), value_ref, n in zip(sets, (value_own_ref, value_oth_ref), (per_row, LANES - per_row)):
        chunks = []
        for c in range(idx_ref.shape[1] // LANES):
            at = slice(part * traps, (part + 1) * traps)
            chunks.append(own_ref[at, :].astype(F32) + got_ref[at, :].astype(F32))
            part += 1
        v = chunks[0] if len(chunks) == 1 else jnp.concatenate(chunks, axis=1)
        within = (idx_ref[...] >= 0) & (idx_ref[...] < rows)
        square = v * v
        amp2 = square + partner(square, n) + 0.25
        ratios.append(jnp.where(within, jnp.sqrt(amp2) * inv_ref[...], 0.0))
        value_ref[...] = jnp.where(within, num_ref[...] / amp2 * v, 0.0)
    own_lanes = lane_of(ratios[0][:, :LANES]) < per_row
    q = jnp.where(own_lanes, ratios[0][:, :LANES], turn(ratios[1][:, :LANES], -per_row)).astype(BF)
    n = LANES - per_row
    back = back_through(scatter(sets[1][0], value_oth_ref, slot_ref, px_ref, n), t_ref, slice(crossing, modes))
    for j in range(n // per_row):
        away_ref[j, :traps, :] = q
        at = traps
        if crossing:
            away_ref[j, at:at + traps, :] = value_oth_ref[...].astype(BF)
            at += traps
        for w in range((modes - crossing) // LANES):
            lanes = slice(w * LANES, (w + 1) * LANES)
            away_ref[j, at:at + per_row, :] = back[j * per_row:(j + 1) * per_row, lanes].astype(BF)
            at += per_row
            away_ref[j, at:at + per_row, :] = back[n + j * per_row:n + (j + 1) * per_row, lanes].astype(BF)
            at += per_row


def mine_kernel(per_row, place_ref, value_ref, idx_ref, slot_ref, t_ref, far_ref, mine_ref, field_ref, px_ref):
    px = field_ref.shape[1]
    own = far_ref[:px, :]
    others = [far_ref[at:at + px, :] for at in range(px, far_ref.shape[0], px)]
    others = others[0] if len(others) == 1 else jnp.concatenate(others, axis=1)
    n = LANES - per_row
    first = lane_of(own) < per_row
    for part in range(2):
        theirs = turn(turn(others, part * n)[:, :LANES], -per_row)
        both = jnp.where(first, turn(own, part * per_row), theirs)
        field_ref[part] = relative(both, place_ref[0], per_row).astype(BF)
    pair = scatter(idx_ref, value_ref, slot_ref, px_ref, per_row)
    mine_ref[...] = back_through(pair, t_ref, slice(None))[:2 * per_row]


def final_kernel(per_row, crossing, place_ref, old_ref, mine_ref, sent_ref, got_ref, *refs):
    n_extra = len(refs) - (7 if crossing else 5)
    slm_ref, weights_ref = refs[n_extra:n_extra + 2]
    out_ref, scaled_ref, sems = refs[-3:]
    traps, count = old_ref.shape
    n_rows = count // per_row
    modes = mine_ref.shape[1]
    q = [sent_ref[0, :traps, :].astype(F32)]
    for m in range(1, n_rows):
        x = got_ref[m - 1, :traps, :].astype(F32)
        for b in range(bits_of(n_rows)):
            if (m >> b) & 1:
                x = flip_blocks(x, per_row, b)
        q.append(x)
    q = tree_sum(q)
    mean = jnp.sum(q, axis=0, keepdims=True) / TRAPS
    scaled_ref[...] = relative(old_ref[...] * mean / q, place_ref[0], per_row)
    copies = [pltpu.make_async_copy(scaled_ref, weights_ref, sems.at[0])]
    copies[0].start()
    scale = jnp.broadcast_to(mean, (count, count)).T[:per_row, 0:1]
    scale = scale * jnp.sqrt(jnp.float32(MODES) / jnp.float32(TRAPS))
    at = traps
    if crossing:
        idx_ref, slot_ref = refs[0:2]
        t_refs = refs[2:n_extra]
        px_ref, value_ref = refs[n_extra + 2:n_extra + 4]
        value_ref[...] = got_ref[0, at:at + traps, :].astype(F32)
        at += traps
        pair = scatter(idx_ref, value_ref, slot_ref, px_ref, per_row)
        across = [back_through(pair, t_ref, slice(None)) for t_ref in t_refs]
    step = 16
    for i in range(per_row // step):
        halves = []
        for part in range(2):
            first = part * per_row + i * step
            total = mine_ref[first:first + step, :]
            theirs = []
            if crossing:
                theirs += [x[first:first + step] for x in across]
            for w in range((modes - crossing) // LANES):
                piece = 0.0
                for m in range(n_rows - 1):
                    piece = piece + got_ref[m, at + 2 * w * per_row + first:at + 2 * w * per_row + first + step, :].astype(F32)
                theirs.append(piece)
            total = total + jnp.concatenate(theirs, axis=1)
            halves.append(total * scale[i * step:(i + 1) * step])
        inv = lax.rsqrt(halves[0] * halves[0] + halves[1] * halves[1] + 1.0)
        for part in range(2):
            out_ref[part, i * step:(i + 1) * step, :] = halves[part] * inv
        piece = pl.ds(i * step, step)
        copies.append(pltpu.make_async_copy(out_ref.at[:, piece, :], slm_ref.at[:, piece, :], sems.at[i + 1]))
        copies[-1].start()
    for copy in copies:
        copy.wait()


def body(transfer, phase, trap_index, levels, weights_old):
    n_rows = lax.axis_size("row")
    n_cols = lax.axis_size("col")
    row = lax.axis_index("row")
    col = lax.axis_index("col")
    rows, modes = transfer.shape[1:]
    count, traps = trap_index.shape
    per_row = count // n_rows
    px = rows // n_cols
    steps = bits_of(n_cols)
    place = jnp.stack([row, col]).astype(jnp.int32)
    masks = [1] + [(1 << b) | 1 for b in range(1, steps)]
    order = []
    for s in range(n_cols):
        j = 0
        for k in range(steps):
            if (s >> (steps - 1 - k)) & 1:
                j ^= masks[k]
        order.append(j)
    wide_own, wide_oth = padded(per_row), padded(count - per_row)
    parts = (wide_own + wide_oth) // LANES
    cuts = [0]
    for piece in CROSS if n_rows == 2 else ():
        cuts.append(cuts[-1] + modes * piece // 8 // LANES * LANES)
    crossing = cuts[-1]

    phase_t = phase.T
    code = jnp.where(phase_t < 0, -1.0, 1.0) * jnp.exp(STEEP * jnp.abs(phase_t))
    code = code.astype(BF)
    others = [swap_pairs(code, m * n_cols) for m in range(1, n_rows)]
    other = others[0] if n_rows == 2 else jnp.concatenate(others, axis=0)
    t_across = []
    for a, b in zip(cuts, cuts[1:]):
        piece = transfer[:, :, a:b]
        if t_across:
            t_across[-1], piece = lax.optimization_barrier((t_across[-1], piece))
        t_across.append(swap_pairs(piece, n_cols))

    cost = dict(flops=1, size=1)
    index, target, old = trap_index.T, levels.T, weights_old.T
    any_space = pl.BlockSpec(memory_space=pl.ANY)
    hbm = pl.BlockSpec(memory_space=pltpu.HBM)
    own_out, own_trap, near = call(
        own_kernel,
        "own",
        [((rows, wide_own), F32), ((traps, wide_own), F32), (transfer.shape, BF)],
        [SMEM, VMEM, VMEM, hbm],
        scratch=[pltpu.SemaphoreType.DMA],
        **cost,
    )(place, phase_t, index, transfer)
    n_half = rows * parts // 2
    n_trap = parts * traps
    keep, send = call(
        functools.partial(other_kernel, order, per_row),
        "other",
        [((n_half, LANES), F32), ((n_half + 2 * n_trap, LANES), BF)],
        [SMEM] + [VMEM] * 5,
        scratch=[pltpu.VMEM((rows, wide_oth), F32)],
        **cost,
    )(place, other, index, near, own_out, own_trap)

    trap = send[n_half:n_half + n_trap].astype(F32) + send[n_half + n_trap:].astype(F32)
    for k in range(steps):
        got = swap_pairs(send, masks[k])
        n = n_half >> k
        total = keep + got[:n].astype(F32)
        if k == steps - 1:
            break
        got_trap = got[n:n + n_trap].astype(F32)
        if k == 0:
            got_trap = got_trap + got[n + n_trap:].astype(F32)
        trap = (trap.astype(F32) + got_trap).astype(BF)
        keep = total[:n // 2]
        send = jnp.concatenate([total[n // 2:].astype(BF), trap], axis=0)
        if k == 0:
            send, index, target, old = lax.optimization_barrier((send, index, target, old))

    tables = [((traps, count), F32)]
    for wide in (wide_own, wide_oth):
        tables += [((traps, wide), jnp.int32), ((traps, wide), F32), ((traps, wide), F32), ((rows, wide), jnp.int32)]
    if crossing:
        tables += [((traps, wide_own), jnp.int32), ((rows, wide_own), jnp.int32)]
    tables = call(
        functools.partial(plan_kernel, per_row, rows, crossing > 0),
        "plan",
        tables,
        [SMEM] + [VMEM] * 3,
        scratch=[pltpu.VMEM((traps, count), jnp.int32)],
        **cost,
    )(place, index, target, old)
    old = tables[0]
    n_away = traps * (2 if crossing else 1) + 2 * per_row * (modes - crossing) // LANES
    value_own, away = call(
        functools.partial(values_kernel, per_row, crossing),
        "values",
        [((traps, wide_own), F32), ((n_rows - 1, n_away, LANES), BF)],
        [VMEM] * 10,
        scratch=[pltpu.VMEM((traps, wide_oth), F32), pltpu.VMEM((rows, wide_oth), F32)],
        **cost,
    )(trap, got[n:], near, *tables[1:4], *tables[5:8], tables[8])
    back = [swap_pairs(away[m - 1], m * n_cols)[None] for m in range(1, n_rows)]
    back = back[0] if n_rows == 2 else jnp.concatenate(back, axis=0)
    mine, field = call(
        functools.partial(mine_kernel, per_row),
        "mine",
        [((2 * per_row, modes), F32), ((2, px, count), BF)],
        [SMEM] + [VMEM] * 5,
        scratch=[pltpu.VMEM((rows, wide_own), F32)],
        **cost,
    )(place, value_own, tables[1], tables[4], near, total)
    extra = [tables[9], tables[10], *t_across] if crossing else []
    room = [pltpu.VMEM((rows, wide_own), F32), pltpu.VMEM((traps, wide_own), F32)] if crossing else []
    slm, weights = call(
        functools.partial(final_kernel, per_row, crossing),
        "final",
        [((2, per_row, modes), F32), ((traps, count), F32)],
        [SMEM] + [VMEM] * (4 + len(extra)),
        out_specs=[any_space, any_space],
        scratch=room
        + [
            pltpu.VMEM((2, per_row, modes), F32),
            pltpu.VMEM((traps, count), F32),
            pltpu.SemaphoreType.DMA((1 + per_row // 16,)),
        ],
        **cost,
    )(place, old, mine, away, back, *extra)

    return jnp.transpose(field, (1, 0, 2)), weights.T, jnp.transpose(slm, (2, 0, 1))


def solution(mesh):
    placed = (P(None, "row", "col"), P("col", "row"), P(), P(), P())
    return jax.shard_map(
        body,
        mesh=mesh,
        in_specs=placed,
        out_specs=(P(("row", "col"), None, None), P(), P("col", None, "row")),
        check_vma=False,
    )
```

```python
import functools

import jax
import jax.numpy as jnp
from jax import lax
from jax.experimental import pallas as pl
from jax.experimental.pallas import tpu as pltpu
from jax.sharding import PartitionSpec as P

MODES = 16384
TRAPS = 64
BF = jnp.bfloat16
F32 = jnp.float32
AXES = ("row", "col")
LANES = 128
SIN = (0.9999996052826214, -0.16666553769418907, 0.008332409691364227, -0.00019808794770261517, 2.6998844729663915e-06,
       -2.0368733379709898e-08)
COS = (0.999999989217114, -0.49999989221470714, 0.041666490704389186, -0.0013887810304225767, 2.4770020037729276e-05,
       -2.708030902998698e-07, 1.7249574387300172e-09)
STEEP = 25.0
NT = (((1,), (1,)), ((), ()))
NN = (((1,), (0,)), ((), ()))
VMEM = pl.BlockSpec(memory_space=pltpu.VMEM)


def call(kernel, name, outs, ins, out_specs=None, scratch=(), flops=0, size=0):
    return pl.pallas_call(
        kernel,
        out_shape=[jax.ShapeDtypeStruct(s, d) for s, d in outs],
        in_specs=ins,
        out_specs=out_specs or [VMEM] * len(outs),
        scratch_shapes=list(scratch),
        compiler_params=pltpu.CompilerParams(vmem_limit_bytes=40 * 1024 * 1024),
        cost_estimate=pl.CostEstimate(flops=flops, bytes_accessed=size, transcendentals=0),
        name=name,
    )


def bits_of(n):
    return n.bit_length() - 1


def padded(n):
    return -(-2 * n // LANES) * LANES


def horner(coefs, y):
    acc = jnp.full_like(y, coefs[-1])
    for c in coefs[-2::-1]:
        acc = acc * y + c
    return acc


def swap_pairs(x, mask):
    n = lax.axis_size("row") * lax.axis_size("col")
    return lax.ppermute(x, AXES, [(i, i ^ mask) for i in range(n)])


def lane_of(x):
    return lax.broadcasted_iota(jnp.int32, x.shape, x.ndim - 1)


def turn(x, by):
    lanes = x.shape[-1]
    by = by % lanes
    return x if by == 0 else pltpu.roll(x, lanes - by, x.ndim - 1)


def flip_blocks(x, width, bit):
    w = width << bit
    return jnp.where((lane_of(x) // w) % 2 == 1, turn(x, -w), turn(x, w))


def spread(x, base, n):
    parts = []
    for c in range(padded(n) // LANES):
        at = LANES * c
        first, second = turn(x, at + base), turn(x, at + base - n)
        parts.append(jnp.where(lane_of(x) + at < n, first, second))
    return parts[0] if len(parts) == 1 else jnp.concatenate(parts, axis=1)


def partner(x, n):
    return jnp.where(lane_of(x) < n, turn(x, n), turn(x, -n))


def tree_sum(parts):
    while len(parts) > 1:
        parts = [parts[i] + parts[i + 1] for i in range(0, len(parts), 2)]
    return parts[0]


def relative(x, row, per_row):
    for b in range(bits_of(x.shape[1] // per_row)):
        x = jnp.where(((row >> b) & 1) == 1, flip_blocks(x, per_row, b), x)
    return x


def project(phase, t_ref, index, out_ref):
    n = phase.shape[0]
    rows = t_ref.shape[1]
    traps, lanes = index.shape
    y = phase * phase
    co = horner(COS, y).astype(BF)
    si = (phase * horner(SIN, y)).astype(BF)
    fill = [jnp.zeros((lanes - 2 * n, phase.shape[1]), BF)] if lanes > 2 * n else []
    out_ref[...] = lax.dot_general(
        t_ref[0], jnp.concatenate([co, si] + fill, axis=0), NT, preferred_element_type=F32
    ) + lax.dot_general(t_ref[1], jnp.concatenate([-si, co] + fill, axis=0), NT, preferred_element_type=F32)
    found = []
    for g in range(traps // 8):
        high = index[g * 8:(g + 1) * 8] >> 3
        low = index[g * 8:(g + 1) * 8] & 7
        got = jnp.zeros((8, lanes), F32)
        for h in range(rows // 8):
            got = jnp.where(high == h, jnp.take_along_axis(out_ref[h * 8:(h + 1) * 8, :], low, axis=0), got)
        found.append(got)
    return found


def own_kernel(ph_ref, index_ref, t_ref, out_ref, trap_ref):
    per_row = ph_ref.shape[0]
    row = lax.axis_index("row")
    index = spread(relative(index_ref[...], row, per_row) - row * t_ref.shape[1], 0, per_row)
    for g, got in enumerate(project(ph_ref[...], t_ref, index, out_ref)):
        trap_ref[g * 8:(g + 1) * 8, :] = got


def other_kernel(order, per_row, code_ref, index_ref, t_ref, own_ref, own_trap_ref, trap_ref, keep_ref, send_ref, out_ref):
    row, col = lax.axis_index("row"), lax.axis_index("col")
    traps, count = index_ref.shape
    rows = t_ref.shape[1]
    index = spread(relative(index_ref[...], row, per_row) - row * rows, per_row, count - per_row)
    code = code_ref[...].astype(F32)
    size = jnp.log(jnp.abs(code)) * (1.0 / STEEP)
    found = project(jnp.where(code < 0, -size, size), t_ref, index, out_ref)
    n_own = own_ref.shape[1] // LANES
    sets = [(own_ref, c) for c in range(n_own)] + [(out_ref, c) for c in range(out_ref.shape[1] // LANES)]
    parts = len(sets)
    for g in range(traps // 8):
        for p, (ref, c) in enumerate(sets):
            lanes = slice(c * LANES, (c + 1) * LANES)
            at = p * traps + g * 8
            trap_ref[at:at + 8, :] = own_trap_ref[g * 8:(g + 1) * 8, lanes] if p < n_own else found[g][:, lanes]
    px = rows // len(order)
    half = len(order) // 2
    for s, j in enumerate(order):
        start = pl.multiple_of((col ^ j) * px, px)
        for p, (ref, c) in enumerate(sets):
            piece = ref[pl.ds(start, px), c * LANES:(c + 1) * LANES]
            at = ((s % half) * parts + p) * px
            if s < half:
                keep_ref[at:at + px, :] = piece
            else:
                send_ref[at:at + px, :] = piece.astype(BF)


def plan_kernel(per_row, rows, index_ref, levels_ref, old_ref, now_ref, *refs):
    row = lax.axis_index("row")
    count = index_ref.shape[1]
    target = relative(levels_ref[...], row, per_row).astype(F32)
    old = relative(old_ref[...], row, per_row)
    mine = relative(index_ref[...], row, per_row) - row * rows
    now_ref[...] = mine
    refs[0][...] = old
    inverse = 1.0 / target
    numer = old * (target * target)
    for s, (base, n) in enumerate(((0, per_row), (per_row, count - per_row))):
        idx_ref, inv_ref, num_ref = refs[1 + 3 * s:4 + 3 * s]
        idx_ref[...] = spread(mine, base, n)
        inv_ref[...] = spread(inverse, base, n)
        num_ref[...] = spread(numer, base, n)


def slot_kernel(per_row, now_ref, *slot_refs):
    traps, count = now_ref.shape
    group = 8

    def find(g, carry):
        start = pl.multiple_of(g * (8 * group), 8 * group)
        pixels = [lax.broadcasted_iota(jnp.int32, (8, count), 0) + (start + 8 * i) for i in range(group)]
        acc = [jnp.full((8, count), -1, jnp.int32) for _ in range(group)]
        for k in range(traps):
            ind = jnp.broadcast_to(now_ref[k:k + 1, :], (8, count))
            for i in range(group):
                acc[i] = jnp.where(ind == pixels[i], k, acc[i])
        for i in range(group):
            for ref, (base, n) in zip(slot_refs, ((0, per_row), (per_row, count - per_row))):
                ref[pl.ds(start + 8 * i, 8), :] = spread(acc[i], base, n)
        return carry

    lax.fori_loop(0, slot_refs[0].shape[0] // (8 * group), find, 0)


def scatter(idx_ref, value_ref, slot_ref, px_ref, n):
    traps, lanes = idx_ref.shape
    index = idx_ref[...]
    acc = [jnp.zeros((8, lanes), F32) for _ in range(traps // 8)]
    for k in range(traps):
        ind = jnp.broadcast_to(idx_ref[k:k + 1, :], (8, lanes))
        val = jnp.broadcast_to(value_ref[k:k + 1, :], (8, lanes))
        for g in range(traps // 8):
            acc[g] += jnp.where(index[g * 8:(g + 1) * 8, :] == ind, val, 0.0)
    for h in range(slot_ref.shape[0] // 8):
        slot = slot_ref[h * 8:(h + 1) * 8, :]
        high = slot >> 3
        low = slot & 7
        got = jnp.zeros((8, lanes), F32)
        for g in range(traps // 8):
            got = jnp.where(high == g, jnp.take_along_axis(acc[g], low, axis=0), got)
        px_ref[h * 8:(h + 1) * 8, :] = got
    proj = px_ref[...].T.astype(BF)
    turned = [proj[n:2 * n], -proj[:n]] + ([proj[2 * n:]] if lanes > 2 * n else [])
    return proj, jnp.concatenate(turned, axis=0)


def back_through(pair, t_ref):
    return lax.dot_general(pair[0], t_ref[0], NN, preferred_element_type=F32) + lax.dot_general(
        pair[1], t_ref[1], NN, preferred_element_type=F32
    )


def values_kernel(per_row, own_ref, got_ref, t_ref, *refs):
    sets = (refs[0:3], refs[3:6])
    slot_ref, value_own_ref, away_ref, value_oth_ref, px_ref = refs[6:]
    rows, modes = t_ref.shape[1:]
    traps = sets[0][0].shape[0]
    ratios = []
    part = 0
    for (idx_ref, inv_ref, num_ref), value_ref, n in zip(sets, (value_own_ref, value_oth_ref), (per_row, LANES - per_row)):
        chunks = []
        for c in range(idx_ref.shape[1] // LANES):
            at = slice(part * traps, (part + 1) * traps)
            chunks.append(own_ref[at, :].astype(F32) + got_ref[at, :].astype(F32))
            part += 1
        v = chunks[0] if len(chunks) == 1 else jnp.concatenate(chunks, axis=1)
        within = (idx_ref[...] >= 0) & (idx_ref[...] < rows)
        square = v * v
        amp2 = square + partner(square, n) + 0.25
        ratios.append(jnp.where(within, jnp.sqrt(amp2) * inv_ref[...], 0.0))
        value_ref[...] = jnp.where(within, num_ref[...] / amp2 * v, 0.0)
    own_lanes = lane_of(ratios[0][:, :LANES]) < per_row
    q = jnp.where(own_lanes, ratios[0][:, :LANES], turn(ratios[1][:, :LANES], -per_row)).astype(BF)
    n = LANES - per_row
    back = back_through(scatter(sets[1][0], value_oth_ref, slot_ref, px_ref, n), t_ref)
    for j in range(n // per_row):
        away_ref[j, :traps, :] = q
        at = traps
        for w in range(modes // LANES):
            lanes = slice(w * LANES, (w + 1) * LANES)
            away_ref[j, at:at + per_row, :] = back[j * per_row:(j + 1) * per_row, lanes].astype(BF)
            at += per_row
            away_ref[j, at:at + per_row, :] = back[n + j * per_row:n + (j + 1) * per_row, lanes].astype(BF)
            at += per_row


def mine_kernel(per_row, value_ref, idx_ref, slot_ref, t_ref, far_ref, mine_ref, field_ref, px_ref):
    px = field_ref.shape[1]
    own = far_ref[:px, :]
    others = [far_ref[at:at + px, :] for at in range(px, far_ref.shape[0], px)]
    others = others[0] if len(others) == 1 else jnp.concatenate(others, axis=1)
    n = LANES - per_row
    first = lane_of(own) < per_row
    for part in range(2):
        theirs = turn(turn(others, part * n)[:, :LANES], -per_row)
        both = jnp.where(first, turn(own, part * per_row), theirs)
        field_ref[part] = relative(both, lax.axis_index("row"), per_row).astype(BF)
    pair = scatter(idx_ref, value_ref, slot_ref, px_ref, per_row)
    mine_ref[...] = back_through(pair, t_ref)[:2 * per_row]


def final_kernel(per_row, old_ref, mine_ref, sent_ref, got_ref, slm_ref, weights_ref, out_ref, scaled_ref, sems):
    traps, count = old_ref.shape
    n_rows = count // per_row
    modes = mine_ref.shape[1]
    q = [sent_ref[0, :traps, :].astype(F32)]
    for m in range(1, n_rows):
        x = got_ref[m - 1, :traps, :].astype(F32)
        for b in range(bits_of(n_rows)):
            if (m >> b) & 1:
                x = flip_blocks(x, per_row, b)
        q.append(x)
    q = tree_sum(q)
    mean = jnp.sum(q, axis=0, keepdims=True) / TRAPS
    scaled_ref[...] = relative(old_ref[...] * mean / q, lax.axis_index("row"), per_row)
    copies = [pltpu.make_async_copy(scaled_ref, weights_ref, sems.at[0])]
    copies[0].start()
    scale = jnp.broadcast_to(mean, (count, count)).T[:per_row, 0:1]
    scale = scale * jnp.sqrt(jnp.float32(MODES) / jnp.float32(TRAPS))
    at = traps
    step = 16
    for i in range(per_row // step):
        halves = []
        for part in range(2):
            first = part * per_row + i * step
            total = mine_ref[first:first + step, :]
            theirs = []
            for w in range(modes // LANES):
                piece = 0.0
                for m in range(n_rows - 1):
                    piece = piece + got_ref[m, at + 2 * w * per_row + first:at + 2 * w * per_row + first + step, :].astype(F32)
                theirs.append(piece)
            total = total + jnp.concatenate(theirs, axis=1)
            halves.append(total * scale[i * step:(i + 1) * step])
        inv = lax.rsqrt(halves[0] * halves[0] + halves[1] * halves[1] + 1.0)
        for part in range(2):
            out_ref[part, i * step:(i + 1) * step, :] = halves[part] * inv
        piece = pl.ds(i * step, step)
        copies.append(pltpu.make_async_copy(out_ref.at[:, piece, :], slm_ref.at[:, piece, :], sems.at[i + 1]))
        copies[-1].start()
    for copy in copies:
        copy.wait()


def body(transfer, phase, trap_index, levels, weights_old):
    n_rows = lax.axis_size("row")
    n_cols = lax.axis_size("col")
    rows, modes = transfer.shape[1:]
    count, traps = trap_index.shape
    per_row = count // n_rows
    px = rows // n_cols
    steps = bits_of(n_cols)
    masks = [1] + [(1 << b) | 1 for b in range(1, steps)]
    order = []
    for s in range(n_cols):
        j = 0
        for k in range(steps):
            if (s >> (steps - 1 - k)) & 1:
                j ^= masks[k]
        order.append(j)
    wide_own, wide_oth = padded(per_row), padded(count - per_row)
    parts = (wide_own + wide_oth) // LANES
    phase_t = phase.T
    code = jnp.where(phase_t < 0, -1.0, 1.0) * jnp.exp(STEEP * jnp.abs(phase_t))
    code = code.astype(BF)
    others = [swap_pairs(code, m * n_cols) for m in range(1, n_rows)]
    other = others[0] if n_rows == 2 else jnp.concatenate(others, axis=0)

    cost = dict(flops=1, size=1)
    index, target, old = trap_index.T, levels.T, weights_old.T
    any_space = pl.BlockSpec(memory_space=pl.ANY)
    sets = (wide_own, wide_oth)
    now, old, *tables = call(
        functools.partial(plan_kernel, per_row, rows),
        "plan",
        [((traps, count), jnp.int32), ((traps, count), F32)]
        + [((traps, wide), d) for wide in sets for d in (jnp.int32, F32, F32)],
        [VMEM] * 3,
        **cost,
    )(index, target, old)

    other, now = lax.optimization_barrier((other, now))
    own_out, own_trap = call(
        own_kernel,
        "own",
        [((rows, wide_own), F32), ((traps, wide_own), F32)],
        [VMEM, VMEM, VMEM],
        **cost,
    )(phase_t, index, transfer)
    n_half = rows * parts // 2
    n_trap = parts * traps
    trap, keep, send = call(
        functools.partial(other_kernel, order, per_row),
        "other",
        [((n_trap, LANES), F32), ((n_half, LANES), F32), ((n_half, LANES), BF)],
        [VMEM] * 5,
        scratch=[pltpu.VMEM((rows, wide_oth), F32)],
        **cost,
    )(other, index, transfer, own_out, own_trap)

    total = trap
    for k in range(steps):
        trap = total if k == 0 else total.astype(BF)
        got = swap_pairs(trap, masks[k])
        total = trap.astype(F32) + got.astype(F32)
        if k == 0:
            total, now = lax.optimization_barrier((total, now))
            slots = call(
                functools.partial(slot_kernel, per_row), "slots", [((rows, wide), jnp.int32) for wide in sets], [VMEM], **cost
            )(now)
        if k == 1:
            total, *slots = lax.optimization_barrier((total, *slots))
    for k in range(steps):
        block = keep + swap_pairs(send, masks[k]).astype(F32)
        half = block.shape[0] // 2
        keep, send = block[:half], block[half:].astype(BF)

    n_away = traps + 2 * per_row * modes // LANES
    value_own, away = call(
        functools.partial(values_kernel, per_row),
        "values",
        [((traps, wide_own), F32), ((n_rows - 1, n_away, LANES), BF)],
        [VMEM] * 10,
        scratch=[pltpu.VMEM((traps, wide_oth), F32), pltpu.VMEM((rows, wide_oth), F32)],
        **cost,
    )(trap, got, transfer, *tables, slots[1])
    back = [swap_pairs(away[m - 1], m * n_cols)[None] for m in range(1, n_rows)]
    back = back[0] if n_rows == 2 else jnp.concatenate(back, axis=0)
    mine, field = call(
        functools.partial(mine_kernel, per_row),
        "mine",
        [((2 * per_row, modes), F32), ((2, px, count), BF)],
        [VMEM] * 5,
        scratch=[pltpu.VMEM((rows, wide_own), F32)],
        **cost,
    )(value_own, tables[0], slots[0], transfer, block)
    slm, weights = call(
        functools.partial(final_kernel, per_row),
        "final",
        [((2, per_row, modes), F32), ((traps, count), F32)],
        [VMEM] * 4,
        out_specs=[any_space, any_space],
        scratch=[
            pltpu.VMEM((2, per_row, modes), F32),
            pltpu.VMEM((traps, count), F32),
            pltpu.SemaphoreType.DMA((1 + per_row // 16,)),
        ],
        **cost,
    )(old, mine, away, back)

    return jnp.transpose(field, (1, 0, 2)), weights.T, jnp.transpose(slm, (2, 0, 1))


def solution(mesh):
    placed = (P(None, "row", "col"), P("col", "row"), P(), P(), P())
    return jax.shard_map(
        body,
        mesh=mesh,
        in_specs=placed,
        out_specs=(P(("row", "col"), None, None), P(), P("col", None, "row")),
        check_vma=False,
    )
```

```python
import functools

import jax
import jax.numpy as jnp
from jax import lax
from jax.experimental import pallas as pl
from jax.experimental.pallas import tpu as pltpu
from jax.sharding import PartitionSpec as P

MODES = 16384
TRAPS = 64
BF = jnp.bfloat16
F32 = jnp.float32
AXES = ("row", "col")
LANES = 128
SIN = (0.9999996052826214, -0.16666553769418907, 0.008332409691364227, -0.00019808794770261517, 2.6998844729663915e-06,
       -2.0368733379709898e-08)
COS = (0.999999989217114, -0.49999989221470714, 0.041666490704389186, -0.0013887810304225767, 2.4770020037729276e-05,
       -2.708030902998698e-07, 1.7249574387300172e-09)
STEEP = 25.0
NT = (((1,), (1,)), ((), ()))
NN = (((1,), (0,)), ((), ()))
VMEM = pl.BlockSpec(memory_space=pltpu.VMEM)


def call(kernel, name, outs, ins, out_specs=None, scratch=(), flops=0, size=0):
    return pl.pallas_call(
        kernel,
        out_shape=[jax.ShapeDtypeStruct(s, d) for s, d in outs],
        in_specs=ins,
        out_specs=out_specs or [VMEM] * len(outs),
        scratch_shapes=list(scratch),
        compiler_params=pltpu.CompilerParams(vmem_limit_bytes=40 * 1024 * 1024),
        cost_estimate=pl.CostEstimate(flops=flops, bytes_accessed=size, transcendentals=0),
        name=name,
    )


def bits_of(n):
    return n.bit_length() - 1


def padded(n):
    return -(-2 * n // LANES) * LANES


def horner(coefs, y):
    acc = jnp.full_like(y, coefs[-1])
    for c in coefs[-2::-1]:
        acc = acc * y + c
    return acc


def swap_pairs(x, mask):
    n = lax.axis_size("row") * lax.axis_size("col")
    return lax.ppermute(x, AXES, [(i, i ^ mask) for i in range(n)])


def lane_of(x):
    return lax.broadcasted_iota(jnp.int32, x.shape, x.ndim - 1)


def turn(x, by):
    lanes = x.shape[-1]
    by = by % lanes
    return x if by == 0 else pltpu.roll(x, lanes - by, x.ndim - 1)


def flip_blocks(x, width, bit):
    w = width << bit
    return jnp.where((lane_of(x) // w) % 2 == 1, turn(x, -w), turn(x, w))


def spread(x, base, n):
    parts = []
    for c in range(padded(n) // LANES):
        at = LANES * c
        first, second = turn(x, at + base), turn(x, at + base - n)
        parts.append(jnp.where(lane_of(x) + at < n, first, second))
    return parts[0] if len(parts) == 1 else jnp.concatenate(parts, axis=1)


def partner(x, n):
    return jnp.where(lane_of(x) < n, turn(x, n), turn(x, -n))


def tree_sum(parts):
    while len(parts) > 1:
        parts = [parts[i] + parts[i + 1] for i in range(0, len(parts), 2)]
    return parts[0]


def relative(x, row, per_row):
    for b in range(bits_of(x.shape[1] // per_row)):
        x = jnp.where(((row >> b) & 1) == 1, flip_blocks(x, per_row, b), x)
    return x


def project(phase, t_ref, index, out_ref):
    n = phase.shape[0]
    rows = t_ref.shape[1]
    traps, lanes = index.shape
    y = phase * phase
    co = horner(COS, y).astype(BF)
    si = (phase * horner(SIN, y)).astype(BF)
    fill = [jnp.zeros((lanes - 2 * n, phase.shape[1]), BF)] if lanes > 2 * n else []
    out_ref[...] = lax.dot_general(
        t_ref[0], jnp.concatenate([co, si] + fill, axis=0), NT, preferred_element_type=F32
    ) + lax.dot_general(t_ref[1], jnp.concatenate([-si, co] + fill, axis=0), NT, preferred_element_type=F32)
    found = []
    for g in range(traps // 8):
        high = index[g * 8:(g + 1) * 8] >> 3
        low = index[g * 8:(g + 1) * 8] & 7
        got = jnp.zeros((8, lanes), F32)
        for h in range(rows // 8):
            got = jnp.where(high == h, jnp.take_along_axis(out_ref[h * 8:(h + 1) * 8, :], low, axis=0), got)
        found.append(got)
    return found


def own_kernel(ph_ref, index_ref, t_ref, out_ref, trap_ref):
    per_row = ph_ref.shape[0]
    row = lax.axis_index("row")
    index = spread(relative(index_ref[...], row, per_row) - row * t_ref.shape[1], 0, per_row)
    for g, got in enumerate(project(ph_ref[...], t_ref, index, out_ref)):
        trap_ref[g * 8:(g + 1) * 8, :] = got


def other_kernel(order, per_row, code_ref, index_ref, t_ref, own_ref, own_trap_ref, trap_ref, keep_ref, send_ref, out_ref):
    row, col = lax.axis_index("row"), lax.axis_index("col")
    traps, count = index_ref.shape
    rows = t_ref.shape[1]
    index = spread(relative(index_ref[...], row, per_row) - row * rows, per_row, count - per_row)
    code = code_ref[...].astype(F32)
    size = jnp.log(jnp.abs(code)) * (1.0 / STEEP)
    found = project(jnp.where(code < 0, -size, size), t_ref, index, out_ref)
    n_own = own_ref.shape[1] // LANES
    sets = [(own_ref, c) for c in range(n_own)] + [(out_ref, c) for c in range(out_ref.shape[1] // LANES)]
    parts = len(sets)
    for g in range(traps // 8):
        for p, (ref, c) in enumerate(sets):
            lanes = slice(c * LANES, (c + 1) * LANES)
            at = p * traps + g * 8
            trap_ref[at:at + 8, :] = own_trap_ref[g * 8:(g + 1) * 8, lanes] if p < n_own else found[g][:, lanes]
    px = rows // len(order)
    half = len(order) // 2
    for s, j in enumerate(order):
        start = pl.multiple_of((col ^ j) * px, px)
        for p, (ref, c) in enumerate(sets):
            piece = ref[pl.ds(start, px), c * LANES:(c + 1) * LANES]
            at = ((s % half) * parts + p) * px
            if s < half:
                keep_ref[at:at + px, :] = piece
            else:
                send_ref[at:at + px, :] = piece.astype(BF)


def plan_kernel(per_row, rows, index_ref, levels_ref, old_ref, now_ref, *refs):
    row = lax.axis_index("row")
    count = index_ref.shape[1]
    target = relative(levels_ref[...], row, per_row).astype(F32)
    old = relative(old_ref[...], row, per_row)
    mine = relative(index_ref[...], row, per_row) - row * rows
    now_ref[...] = mine
    refs[0][...] = old
    inverse = 1.0 / target
    numer = old * (target * target)
    for s, (base, n) in enumerate(((0, per_row), (per_row, count - per_row))):
        idx_ref, inv_ref, num_ref = refs[1 + 3 * s:4 + 3 * s]
        idx_ref[...] = spread(mine, base, n)
        inv_ref[...] = spread(inverse, base, n)
        num_ref[...] = spread(numer, base, n)


def slot_kernel(per_row, now_ref, *slot_refs):
    traps, count = now_ref.shape
    group = 8

    def find(g, carry):
        start = pl.multiple_of(g * (8 * group), 8 * group)
        pixels = [lax.broadcasted_iota(jnp.int32, (8, count), 0) + (start + 8 * i) for i in range(group)]
        acc = [jnp.full((8, count), -1, jnp.int32) for _ in range(group)]
        for k in range(traps):
            ind = jnp.broadcast_to(now_ref[k:k + 1, :], (8, count))
            for i in range(group):
                acc[i] = jnp.where(ind == pixels[i], k, acc[i])
        for i in range(group):
            for ref, (base, n) in zip(slot_refs, ((0, per_row), (per_row, count - per_row))):
                ref[pl.ds(start + 8 * i, 8), :] = spread(acc[i], base, n)
        return carry

    lax.fori_loop(0, slot_refs[0].shape[0] // (8 * group), find, 0)


def scatter(idx_ref, value_ref, slot_ref, px_ref, n):
    traps, lanes = idx_ref.shape
    index = idx_ref[...]
    acc = [jnp.zeros((8, lanes), F32) for _ in range(traps // 8)]
    for k in range(traps):
        ind = jnp.broadcast_to(idx_ref[k:k + 1, :], (8, lanes))
        val = jnp.broadcast_to(value_ref[k:k + 1, :], (8, lanes))
        for g in range(traps // 8):
            acc[g] += jnp.where(index[g * 8:(g + 1) * 8, :] == ind, val, 0.0)
    for h in range(slot_ref.shape[0] // 8):
        slot = slot_ref[h * 8:(h + 1) * 8, :]
        high = slot >> 3
        low = slot & 7
        got = jnp.zeros((8, lanes), F32)
        for g in range(traps // 8):
            got = jnp.where(high == g, jnp.take_along_axis(acc[g], low, axis=0), got)
        px_ref[h * 8:(h + 1) * 8, :] = got
    proj = px_ref[...].T.astype(BF)
    turned = [proj[n:2 * n], -proj[:n]] + ([proj[2 * n:]] if lanes > 2 * n else [])
    return proj, jnp.concatenate(turned, axis=0)


def back_through(pair, t_ref):
    return lax.dot_general(pair[0], t_ref[0], NN, preferred_element_type=F32) + lax.dot_general(
        pair[1], t_ref[1], NN, preferred_element_type=F32
    )


def values_kernel(per_row, trap_ref, t_ref, *refs):
    sets = (refs[0:3], refs[3:6])
    slot_ref, value_own_ref, away_ref, value_oth_ref, px_ref = refs[6:]
    rows, modes = t_ref.shape[1:]
    traps = sets[0][0].shape[0]
    ratios = []
    part = 0
    for (idx_ref, inv_ref, num_ref), value_ref, n in zip(sets, (value_own_ref, value_oth_ref), (per_row, LANES - per_row)):
        chunks = []
        for c in range(idx_ref.shape[1] // LANES):
            at = slice(part * traps, (part + 1) * traps)
            chunks.append(trap_ref[at, :])
            part += 1
        v = chunks[0] if len(chunks) == 1 else jnp.concatenate(chunks, axis=1)
        within = (idx_ref[...] >= 0) & (idx_ref[...] < rows)
        square = v * v
        amp2 = square + partner(square, n) + 0.25
        ratios.append(jnp.where(within, jnp.sqrt(amp2) * inv_ref[...], 0.0))
        value_ref[...] = jnp.where(within, num_ref[...] / amp2 * v, 0.0)
    own_lanes = lane_of(ratios[0][:, :LANES]) < per_row
    q = jnp.where(own_lanes, ratios[0][:, :LANES], turn(ratios[1][:, :LANES], -per_row)).astype(BF)
    n = LANES - per_row
    back = back_through(scatter(sets[1][0], value_oth_ref, slot_ref, px_ref, n), t_ref)
    for j in range(n // per_row):
        away_ref[j, :traps, :] = q
        at = traps
        for w in range(modes // LANES):
            lanes = slice(w * LANES, (w + 1) * LANES)
            away_ref[j, at:at + per_row, :] = back[j * per_row:(j + 1) * per_row, lanes].astype(BF)
            at += per_row
            away_ref[j, at:at + per_row, :] = back[n + j * per_row:n + (j + 1) * per_row, lanes].astype(BF)
            at += per_row


def mine_kernel(per_row, value_ref, idx_ref, slot_ref, t_ref, far_ref, mine_ref, field_ref, px_ref):
    px = field_ref.shape[1]
    own = far_ref[:px, :]
    others = [far_ref[at:at + px, :] for at in range(px, far_ref.shape[0], px)]
    others = others[0] if len(others) == 1 else jnp.concatenate(others, axis=1)
    n = LANES - per_row
    first = lane_of(own) < per_row
    for part in range(2):
        theirs = turn(turn(others, part * n)[:, :LANES], -per_row)
        both = jnp.where(first, turn(own, part * per_row), theirs)
        field_ref[part] = relative(both, lax.axis_index("row"), per_row).astype(BF)
    pair = scatter(idx_ref, value_ref, slot_ref, px_ref, per_row)
    mine_ref[...] = back_through(pair, t_ref)[:2 * per_row]


def final_kernel(per_row, old_ref, mine_ref, sent_ref, got_ref, slm_ref, weights_ref, out_ref, scaled_ref, sems):
    traps, count = old_ref.shape
    n_rows = count // per_row
    modes = mine_ref.shape[1]
    q = [sent_ref[0, :traps, :].astype(F32)]
    for m in range(1, n_rows):
        x = got_ref[m - 1, :traps, :].astype(F32)
        for b in range(bits_of(n_rows)):
            if (m >> b) & 1:
                x = flip_blocks(x, per_row, b)
        q.append(x)
    q = tree_sum(q)
    mean = jnp.sum(q, axis=0, keepdims=True) / TRAPS
    scaled_ref[...] = relative(old_ref[...] * mean / q, lax.axis_index("row"), per_row)
    copies = [pltpu.make_async_copy(scaled_ref, weights_ref, sems.at[0])]
    copies[0].start()
    scale = jnp.broadcast_to(mean, (count, count)).T[:per_row, 0:1]
    scale = scale * jnp.sqrt(jnp.float32(MODES) / jnp.float32(TRAPS))
    at = traps
    step = 16
    for i in range(per_row // step):
        halves = []
        for part in range(2):
            first = part * per_row + i * step
            total = mine_ref[first:first + step, :]
            theirs = []
            for w in range(modes // LANES):
                piece = 0.0
                for m in range(n_rows - 1):
                    piece = piece + got_ref[m, at + 2 * w * per_row + first:at + 2 * w * per_row + first + step, :].astype(F32)
                theirs.append(piece)
            total = total + jnp.concatenate(theirs, axis=1)
            halves.append(total * scale[i * step:(i + 1) * step])
        inv = lax.rsqrt(halves[0] * halves[0] + halves[1] * halves[1] + 1.0)
        for part in range(2):
            out_ref[part, i * step:(i + 1) * step, :] = halves[part] * inv
        piece = pl.ds(i * step, step)
        copies.append(pltpu.make_async_copy(out_ref.at[:, piece, :], slm_ref.at[:, piece, :], sems.at[i + 1]))
        copies[-1].start()
    for copy in copies:
        copy.wait()


def body(transfer, phase, trap_index, levels, weights_old):
    n_rows = lax.axis_size("row")
    n_cols = lax.axis_size("col")
    rows, modes = transfer.shape[1:]
    count, traps = trap_index.shape
    per_row = count // n_rows
    px = rows // n_cols
    steps = bits_of(n_cols)
    masks = [1] + [(1 << b) | 1 for b in range(1, steps)]
    order = []
    for s in range(n_cols):
        j = 0
        for k in range(steps):
            if (s >> (steps - 1 - k)) & 1:
                j ^= masks[k]
        order.append(j)
    wide_own, wide_oth = padded(per_row), padded(count - per_row)
    parts = (wide_own + wide_oth) // LANES
    phase_t = phase.T
    code = jnp.where(phase_t < 0, -1.0, 1.0) * jnp.exp(STEEP * jnp.abs(phase_t))
    code = code.astype(BF)
    others = [swap_pairs(code, m * n_cols) for m in range(1, n_rows)]
    other = others[0] if n_rows == 2 else jnp.concatenate(others, axis=0)

    cost = dict(flops=1, size=1)
    index, target, old = trap_index.T, levels.T, weights_old.T
    any_space = pl.BlockSpec(memory_space=pl.ANY)
    sets = (wide_own, wide_oth)
    now, old, *tables = call(
        functools.partial(plan_kernel, per_row, rows),
        "plan",
        [((traps, count), jnp.int32), ((traps, count), F32)]
        + [((traps, wide), d) for wide in sets for d in (jnp.int32, F32, F32)],
        [VMEM] * 3,
        **cost,
    )(index, target, old)

    other, now = lax.optimization_barrier((other, now))
    own_out, own_trap = call(
        own_kernel,
        "own",
        [((rows, wide_own), F32), ((traps, wide_own), F32)],
        [VMEM, VMEM, VMEM],
        **cost,
    )(phase_t, index, transfer)
    n_half = rows * parts // 2
    n_trap = parts * traps
    trap, keep, send = call(
        functools.partial(other_kernel, order, per_row),
        "other",
        [((n_trap, LANES), F32), ((n_half, LANES), F32), ((n_half, LANES), BF)],
        [VMEM] * 5,
        scratch=[pltpu.VMEM((rows, wide_oth), F32)],
        **cost,
    )(other, index, transfer, own_out, own_trap)

    trap = trap + swap_pairs(trap, 1)
    trap, now = lax.optimization_barrier((trap, now))
    slots = call(
        functools.partial(slot_kernel, per_row), "slots", [((rows, wide), jnp.int32) for wide in sets], [VMEM], **cost
    )(now)
    for group in (range(1, min(3, steps)), *[[b] for b in range(3, steps)]):
        short = trap.astype(BF)
        chips = [0]
        for b in group:
            chips += [m | 1 << b for m in chips]
        got = [swap_pairs(short, m | 1) if m else short for m in chips]
        trap = tree_sum([x.astype(F32) for x in got])
        if group[0] == 1:
            trap, *slots = lax.optimization_barrier((trap, *slots))
    for k in range(steps):
        block = keep + swap_pairs(send, masks[k]).astype(F32)
        half = block.shape[0] // 2
        keep, send = block[:half], block[half:].astype(BF)

    n_away = traps + 2 * per_row * modes // LANES
    value_own, away = call(
        functools.partial(values_kernel, per_row),
        "values",
        [((traps, wide_own), F32), ((n_rows - 1, n_away, LANES), BF)],
        [VMEM] * 9,
        scratch=[pltpu.VMEM((traps, wide_oth), F32), pltpu.VMEM((rows, wide_oth), F32)],
        **cost,
    )(trap, transfer, *tables, slots[1])
    back = [swap_pairs(away[m - 1], m * n_cols)[None] for m in range(1, n_rows)]
    back = back[0] if n_rows == 2 else jnp.concatenate(back, axis=0)
    mine, field = call(
        functools.partial(mine_kernel, per_row),
        "mine",
        [((2 * per_row, modes), F32), ((2, px, count), BF)],
        [VMEM] * 5,
        scratch=[pltpu.VMEM((rows, wide_own), F32)],
        **cost,
    )(value_own, tables[0], slots[0], transfer, block)
    slm, weights = call(
        functools.partial(final_kernel, per_row),
        "final",
        [((2, per_row, modes), F32), ((traps, count), F32)],
        [VMEM] * 4,
        out_specs=[any_space, any_space],
        scratch=[
            pltpu.VMEM((2, per_row, modes), F32),
            pltpu.VMEM((traps, count), F32),
            pltpu.SemaphoreType.DMA((1 + per_row // 16,)),
        ],
        **cost,
    )(old, mine, away, back)

    return jnp.transpose(field, (1, 0, 2)), weights.T, jnp.transpose(slm, (2, 0, 1))


def solution(mesh):
    placed = (P(None, "row", "col"), P("col", "row"), P(), P(), P())
    return jax.shard_map(
        body,
        mesh=mesh,
        in_specs=placed,
        out_specs=(P(("row", "col"), None, None), P(), P("col", None, "row")),
        check_vma=False,
    )
```

```python
import functools

import jax
import jax.numpy as jnp
from jax import lax
from jax.experimental import pallas as pl
from jax.experimental.pallas import tpu as pltpu
from jax.sharding import PartitionSpec as P

MODES = 16384
TRAPS = 64
BF = jnp.bfloat16
F32 = jnp.float32
AXES = ("row", "col")
LANES = 128
SIN = (0.9999996052826214, -0.16666553769418907, 0.008332409691364227, -0.00019808794770261517, 2.6998844729663915e-06,
       -2.0368733379709898e-08)
COS = (0.999999989217114, -0.49999989221470714, 0.041666490704389186, -0.0013887810304225767, 2.4770020037729276e-05,
       -2.708030902998698e-07, 1.7249574387300172e-09)
STEEP = 25.0
CROSS = 6
NT = (((1,), (1,)), ((), ()))
NN = (((1,), (0,)), ((), ()))
VMEM = pl.BlockSpec(memory_space=pltpu.VMEM)


def call(kernel, name, outs, ins, out_specs=None, scratch=(), flops=0, size=0):
    return pl.pallas_call(
        kernel,
        out_shape=[jax.ShapeDtypeStruct(s, d) for s, d in outs],
        in_specs=ins,
        out_specs=out_specs or [VMEM] * len(outs),
        scratch_shapes=list(scratch),
        compiler_params=pltpu.CompilerParams(vmem_limit_bytes=40 * 1024 * 1024),
        cost_estimate=pl.CostEstimate(flops=flops, bytes_accessed=size, transcendentals=0),
        name=name,
    )


def bits_of(n):
    return n.bit_length() - 1


def padded(n):
    return -(-2 * n // LANES) * LANES


def horner(coefs, y):
    acc = jnp.full_like(y, coefs[-1])
    for c in coefs[-2::-1]:
        acc = acc * y + c
    return acc


def swap_pairs(x, mask):
    n = lax.axis_size("row") * lax.axis_size("col")
    return lax.ppermute(x, AXES, [(i, i ^ mask) for i in range(n)])


def lane_of(x):
    return lax.broadcasted_iota(jnp.int32, x.shape, x.ndim - 1)


def turn(x, by):
    lanes = x.shape[-1]
    by = by % lanes
    return x if by == 0 else pltpu.roll(x, lanes - by, x.ndim - 1)


def flip_blocks(x, width, bit):
    w = width << bit
    return jnp.where((lane_of(x) // w) % 2 == 1, turn(x, -w), turn(x, w))


def spread(x, base, n):
    parts = []
    for c in range(padded(n) // LANES):
        at = LANES * c
        first, second = turn(x, at + base), turn(x, at + base - n)
        parts.append(jnp.where(lane_of(x) + at < n, first, second))
    return parts[0] if len(parts) == 1 else jnp.concatenate(parts, axis=1)


def partner(x, n):
    return jnp.where(lane_of(x) < n, turn(x, n), turn(x, -n))


def tree_sum(parts):
    while len(parts) > 1:
        parts = [parts[i] + parts[i + 1] for i in range(0, len(parts), 2)]
    return parts[0]


def relative(x, row, per_row):
    for b in range(bits_of(x.shape[1] // per_row)):
        x = jnp.where(((row >> b) & 1) == 1, flip_blocks(x, per_row, b), x)
    return x


def project(phase, t_ref, index, out_ref):
    n = phase.shape[0]
    rows = t_ref.shape[1]
    traps, lanes = index.shape
    y = phase * phase
    co = horner(COS, y).astype(BF)
    si = (phase * horner(SIN, y)).astype(BF)
    fill = [jnp.zeros((lanes - 2 * n, phase.shape[1]), BF)] if lanes > 2 * n else []
    out_ref[...] = lax.dot_general(
        t_ref[0], jnp.concatenate([co, si] + fill, axis=0), NT, preferred_element_type=F32
    ) + lax.dot_general(t_ref[1], jnp.concatenate([-si, co] + fill, axis=0), NT, preferred_element_type=F32)
    found = []
    for g in range(traps // 8):
        high = index[g * 8:(g + 1) * 8] >> 3
        low = index[g * 8:(g + 1) * 8] & 7
        got = jnp.zeros((8, lanes), F32)
        for h in range(rows // 8):
            got = jnp.where(high == h, jnp.take_along_axis(out_ref[h * 8:(h + 1) * 8, :], low, axis=0), got)
        found.append(got)
    return found


def own_kernel(ph_ref, index_ref, t_ref, out_ref, trap_ref):
    per_row = ph_ref.shape[0]
    row = lax.axis_index("row")
    index = spread(relative(index_ref[...], row, per_row) - row * t_ref.shape[1], 0, per_row)
    for g, got in enumerate(project(ph_ref[...], t_ref, index, out_ref)):
        trap_ref[g * 8:(g + 1) * 8, :] = got


def other_kernel(order, per_row, code_ref, index_ref, t_ref, own_ref, own_trap_ref, trap_ref, keep_ref, send_ref, out_ref):
    row, col = lax.axis_index("row"), lax.axis_index("col")
    traps, count = index_ref.shape
    rows = t_ref.shape[1]
    index = spread(relative(index_ref[...], row, per_row) - row * rows, per_row, count - per_row)
    code = code_ref[...].astype(F32)
    size = jnp.log(jnp.abs(code)) * (1.0 / STEEP)
    found = project(jnp.where(code < 0, -size, size), t_ref, index, out_ref)
    n_own = own_ref.shape[1] // LANES
    sets = [(own_ref, c) for c in range(n_own)] + [(out_ref, c) for c in range(out_ref.shape[1] // LANES)]
    parts = len(sets)
    for g in range(traps // 8):
        for p, (ref, c) in enumerate(sets):
            lanes = slice(c * LANES, (c + 1) * LANES)
            at = p * traps + g * 8
            trap_ref[at:at + 8, :] = own_trap_ref[g * 8:(g + 1) * 8, lanes] if p < n_own else found[g][:, lanes]
    px = rows // len(order)
    half = len(order) // 2
    for s, j in enumerate(order):
        start = pl.multiple_of((col ^ j) * px, px)
        for p, (ref, c) in enumerate(sets):
            piece = ref[pl.ds(start, px), c * LANES:(c + 1) * LANES]
            at = ((s % half) * parts + p) * px
            if s < half:
                keep_ref[at:at + px, :] = piece
            else:
                send_ref[at:at + px, :] = piece.astype(BF)


def plan_kernel(per_row, rows, index_ref, levels_ref, old_ref, now_ref, *refs):
    row = lax.axis_index("row")
    count = index_ref.shape[1]
    target = relative(levels_ref[...], row, per_row).astype(F32)
    old = relative(old_ref[...], row, per_row)
    mine = relative(index_ref[...], row, per_row) - row * rows
    now_ref[...] = mine
    refs[0][...] = old
    theirs = mine + (2 * row - 1) * rows
    refs[-2][...] = theirs
    refs[-1][...] = spread(theirs, 0, per_row)
    inverse = 1.0 / target
    numer = old * (target * target)
    for s, (base, n) in enumerate(((0, per_row), (per_row, count - per_row))):
        idx_ref, inv_ref, num_ref = refs[1 + 3 * s:4 + 3 * s]
        idx_ref[...] = spread(mine, base, n)
        inv_ref[...] = spread(inverse, base, n)
        num_ref[...] = spread(numer, base, n)


def slot_kernel(sets, now_ref, *slot_refs):
    traps, count = now_ref.shape
    group = 8

    def find(g, carry):
        start = pl.multiple_of(g * (8 * group), 8 * group)
        pixels = [lax.broadcasted_iota(jnp.int32, (8, count), 0) + (start + 8 * i) for i in range(group)]
        acc = [jnp.full((8, count), -1, jnp.int32) for _ in range(group)]
        for k in range(traps):
            ind = jnp.broadcast_to(now_ref[k:k + 1, :], (8, count))
            for i in range(group):
                acc[i] = jnp.where(ind == pixels[i], k, acc[i])
        for i in range(group):
            for ref, (base, n) in zip(slot_refs, sets):
                ref[pl.ds(start + 8 * i, 8), :] = spread(acc[i], base, n)
        return carry

    lax.fori_loop(0, slot_refs[0].shape[0] // (8 * group), find, 0)


def scatter(idx_ref, value_ref, slot_ref, px_ref, n):
    traps, lanes = idx_ref.shape
    index = idx_ref[...]
    acc = [jnp.zeros((8, lanes), F32) for _ in range(traps // 8)]
    for k in range(traps):
        ind = jnp.broadcast_to(idx_ref[k:k + 1, :], (8, lanes))
        val = jnp.broadcast_to(value_ref[k:k + 1, :], (8, lanes))
        for g in range(traps // 8):
            acc[g] += jnp.where(index[g * 8:(g + 1) * 8, :] == ind, val, 0.0)
    for h in range(slot_ref.shape[0] // 8):
        slot = slot_ref[h * 8:(h + 1) * 8, :]
        high = slot >> 3
        low = slot & 7
        got = jnp.zeros((8, lanes), F32)
        for g in range(traps // 8):
            got = jnp.where(high == g, jnp.take_along_axis(acc[g], low, axis=0), got)
        px_ref[h * 8:(h + 1) * 8, :] = got
    proj = px_ref[...].astype(BF).T
    turned = [proj[n:2 * n], -proj[:n]] + ([proj[2 * n:]] if lanes > 2 * n else [])
    return proj, jnp.concatenate(turned, axis=0)


def back_through(pair, t_ref, first, last):
    return lax.dot_general(pair[0], t_ref[0, :, first:last], NN, preferred_element_type=F32) + lax.dot_general(
        pair[1], t_ref[1, :, first:last], NN, preferred_element_type=F32
    )


def values_kernel(per_row, crossing, trap_ref, t_ref, *refs):
    sets = (refs[0:3], refs[3:6])
    slot_ref, value_own_ref, away_ref, value_oth_ref, px_ref = refs[6:]
    rows, modes = t_ref.shape[1:]
    traps = sets[0][0].shape[0]
    ratios = []
    part = 0
    for (idx_ref, inv_ref, num_ref), value_ref, n in zip(sets, (value_own_ref, value_oth_ref), (per_row, LANES - per_row)):
        chunks = []
        for c in range(idx_ref.shape[1] // LANES):
            at = slice(part * traps, (part + 1) * traps)
            chunks.append(trap_ref[at, :])
            part += 1
        v = chunks[0] if len(chunks) == 1 else jnp.concatenate(chunks, axis=1)
        within = (idx_ref[...] >= 0) & (idx_ref[...] < rows)
        square = v * v
        amp2 = square + partner(square, n) + 0.25
        ratios.append(jnp.where(within, jnp.sqrt(amp2) * inv_ref[...], 0.0))
        value_ref[...] = jnp.where(within, num_ref[...] / amp2 * v, 0.0)
    own_lanes = lane_of(ratios[0][:, :LANES]) < per_row
    q = jnp.where(own_lanes, ratios[0][:, :LANES], turn(ratios[1][:, :LANES], -per_row)).astype(BF)
    n = LANES - per_row
    back = back_through(scatter(sets[1][0], value_oth_ref, slot_ref, px_ref, n), t_ref, crossing, modes)
    for j in range(n // per_row):
        away_ref[j, :traps, :] = q
        at = traps
        if crossing:
            away_ref[j, at:at + traps, :] = value_oth_ref[...].astype(BF)
            at += traps
        for w in range((modes - crossing) // LANES):
            lanes = slice(w * LANES, (w + 1) * LANES)
            away_ref[j, at:at + per_row, :] = back[j * per_row:(j + 1) * per_row, lanes].astype(BF)
            at += per_row
            away_ref[j, at:at + per_row, :] = back[n + j * per_row:n + (j + 1) * per_row, lanes].astype(BF)
            at += per_row


def far_kernel(per_row, far_ref, field_ref):
    px = field_ref.shape[1]
    own = far_ref[:px, :]
    others = [far_ref[at:at + px, :] for at in range(px, far_ref.shape[0], px)]
    others = others[0] if len(others) == 1 else jnp.concatenate(others, axis=1)
    n = LANES - per_row
    first = lane_of(own) < per_row
    for part in range(2):
        theirs = turn(turn(others, part * n)[:, :LANES], -per_row)
        both = jnp.where(first, turn(own, part * per_row), theirs)
        field_ref[part] = relative(both, lax.axis_index("row"), per_row).astype(BF)


def mine_kernel(per_row, value_ref, idx_ref, slot_ref, t_ref, mine_ref, px_ref):
    pair = scatter(idx_ref, value_ref, slot_ref, px_ref, per_row)
    mine_ref[...] = back_through(pair, t_ref, 0, t_ref.shape[2])[:2 * per_row]


def final_kernel(per_row, crossing, old_ref, mine_ref, sent_ref, got_ref, *refs):
    slm_ref, weights_ref, out_ref, scaled_ref, sems = refs[3:8] if crossing else refs
    traps, count = old_ref.shape
    n_rows = count // per_row
    modes = mine_ref.shape[1]
    q = [sent_ref[0, :traps, :].astype(F32)]
    for m in range(1, n_rows):
        x = got_ref[m - 1, :traps, :].astype(F32)
        for b in range(bits_of(n_rows)):
            if (m >> b) & 1:
                x = flip_blocks(x, per_row, b)
        q.append(x)
    q = tree_sum(q)
    mean = jnp.sum(q, axis=0, keepdims=True) / TRAPS
    copies = []
    scale = jnp.broadcast_to(mean, (count, count)).T[:per_row, 0:1]
    scale = scale * jnp.sqrt(jnp.float32(MODES) / jnp.float32(TRAPS))
    at = traps
    across = []
    if crossing:
        idx_ref, slot_ref, t_ref = refs[:3]
        px_ref, value_ref = refs[8:]
        value_ref[...] = got_ref[0, at:at + traps, :].astype(F32)
        at += traps
        across = [back_through(scatter(idx_ref, value_ref, slot_ref, px_ref, per_row), t_ref, 0, crossing)]
    step = 16
    for i in range(per_row // step):
        halves = []
        for part in range(2):
            first = part * per_row + i * step
            total = mine_ref[first:first + step, :]
            theirs = [x[first:first + step] for x in across]
            for w in range((modes - crossing) // LANES):
                piece = 0.0
                for m in range(n_rows - 1):
                    piece = piece + got_ref[m, at + 2 * w * per_row + first:at + 2 * w * per_row + first + step, :].astype(F32)
                theirs.append(piece)
            total = total + jnp.concatenate(theirs, axis=1)
            halves.append(total * scale[i * step:(i + 1) * step])
        inv = lax.rsqrt(halves[0] * halves[0] + halves[1] * halves[1] + 1.0)
        for part in range(2):
            out_ref[part, i * step:(i + 1) * step, :] = halves[part] * inv
        piece = pl.ds(i * step, step)
        copies.append(pltpu.make_async_copy(out_ref.at[:, piece, :], slm_ref.at[:, piece, :], sems.at[i + 1]))
        copies[-1].start()
        if i == 0:
            scaled_ref[...] = relative(old_ref[...] * mean / q, lax.axis_index("row"), per_row)
            copies.append(pltpu.make_async_copy(scaled_ref, weights_ref, sems.at[0]))
            copies[-1].start()
    for copy in copies:
        copy.wait()


def body(transfer, phase, trap_index, levels, weights_old):
    n_rows = lax.axis_size("row")
    n_cols = lax.axis_size("col")
    rows, modes = transfer.shape[1:]
    count, traps = trap_index.shape
    per_row = count // n_rows
    px = rows // n_cols
    steps = bits_of(n_cols)
    masks = [1] + [(1 << b) | 1 for b in range(1, steps)]
    order = []
    for s in range(n_cols):
        j = 0
        for k in range(steps):
            if (s >> (steps - 1 - k)) & 1:
                j ^= masks[k]
        order.append(j)
    wide_own, wide_oth = padded(per_row), padded(count - per_row)
    parts = (wide_own + wide_oth) // LANES
    crossing = modes * CROSS // 8 // LANES * LANES if n_rows == 2 else 0
    phase_t = phase.T
    code = jnp.where(phase_t < 0, -1.0, 1.0) * jnp.exp(STEEP * jnp.abs(phase_t))
    code = code.astype(BF)
    others = [swap_pairs(code, m * n_cols) for m in range(1, n_rows)]
    other = others[0] if n_rows == 2 else jnp.concatenate(others, axis=0)

    cost = dict(flops=1, size=1)
    index, target, old = trap_index.T, levels.T, weights_old.T
    any_space = pl.BlockSpec(memory_space=pl.ANY)
    sets = (wide_own, wide_oth)
    now, old, *tables, now_cross, idx_cross = call(
        functools.partial(plan_kernel, per_row, rows),
        "plan",
        [((traps, count), jnp.int32), ((traps, count), F32)]
        + [((traps, wide), d) for wide in sets for d in (jnp.int32, F32, F32)]
        + [((traps, count), jnp.int32), ((traps, wide_own), jnp.int32)],
        [VMEM] * 3,
        **cost,
    )(index, target, old)

    if crossing:
        t_across = swap_pairs(transfer[:, :, :crossing], n_cols)
    other, now = lax.optimization_barrier((other, now))
    own_out, own_trap = call(
        own_kernel,
        "own",
        [((rows, wide_own), F32), ((traps, wide_own), F32)],
        [VMEM, VMEM, VMEM],
        **cost,
    )(phase_t, index, transfer)
    n_half = rows * parts // 2
    n_trap = parts * traps
    trap, keep, send = call(
        functools.partial(other_kernel, order, per_row),
        "other",
        [((n_trap, LANES), F32), ((n_half, LANES), F32), ((n_half, LANES), BF)],
        [VMEM] * 5,
        scratch=[pltpu.VMEM((rows, wide_oth), F32)],
        flops=3 * 10**10,
        size=1,
    )(other, index, transfer, own_out, own_trap)

    own_set, oth_set = (0, per_row), (per_row, count - per_row)

    def plan_slots(now, *which):
        return call(
            functools.partial(slot_kernel, which),
            "slots",
            [((rows, padded(n)), jnp.int32) for _, n in which],
            [VMEM],
            **cost,
        )(now)

    groups = [list(range(1, min(3, steps)))] + [[b] for b in range(3, steps)]

    def sums(trap, keep, send, now):
        block = keep + swap_pairs(send, masks[0]).astype(F32)
        trap = trap + swap_pairs(trap, masks[0])
        trap, now = lax.optimization_barrier((trap, now))
        slots = plan_slots(now, own_set, oth_set)
        for group in groups:
            short = trap.astype(BF)
            ways = 1 << len(group)
            part = block.shape[0] // ways
            whole = block
            fields, traps_of = [whole[:part]], [short]
            for way in range(1, ways):
                mask = 0
                for i, b in enumerate(group):
                    if (way >> (len(group) - 1 - i)) & 1:
                        mask ^= masks[b]
                load = jnp.concatenate([short, whole[way * part:(way + 1) * part].astype(BF)], axis=0)
                got = swap_pairs(load, mask)
                traps_of.append(got[:short.shape[0]])
                fields.append(got[short.shape[0]:])
            trap = tree_sum([x.astype(F32) for x in traps_of])
            block = tree_sum([x.astype(F32) for x in fields])
            if group[0] == 1:
                trap, *slots = lax.optimization_barrier((trap, *slots))
        return (trap, block, *slots)

    if crossing:
        shapes = jax.eval_shape(sums, trap, keep, send, now)
        trap, block, *slots = lax.cond(
            trap_index[0, 0] >= 0, sums, lambda *args: tuple(jnp.zeros(x.shape, x.dtype) for x in shapes), trap, keep, send, now
        )
    else:
        trap, block, *slots = sums(trap, keep, send, now)

    n_away = traps * (2 if crossing else 1) + 2 * per_row * (modes - crossing) // LANES
    value_own, away = call(
        functools.partial(values_kernel, per_row, crossing),
        "values",
        [((traps, wide_own), F32), ((n_rows - 1, n_away, LANES), BF)],
        [VMEM] * 9,
        scratch=[pltpu.VMEM((traps, wide_oth), F32), pltpu.VMEM((rows, wide_oth), F32)],
        **cost,
    )(trap, transfer, *tables, slots[1])
    back = [swap_pairs(away[m - 1], m * n_cols)[None] for m in range(1, n_rows)]
    back = back[0] if n_rows == 2 else jnp.concatenate(back, axis=0)
    (field,) = call(functools.partial(far_kernel, per_row), "far", [((2, px, count), BF)], [VMEM], **cost)(block)
    (mine,) = call(
        functools.partial(mine_kernel, per_row),
        "mine",
        [((2 * per_row, modes), F32)],
        [VMEM] * 4,
        scratch=[pltpu.VMEM((rows, wide_own), F32)],
        **cost,
    )(value_own, tables[0], slots[0], transfer)
    if crossing:
        mine, now_cross = lax.optimization_barrier((mine, now_cross))
        (slots_cross,) = plan_slots(now_cross, own_set)
    extra = [idx_cross, slots_cross, t_across] if crossing else []
    room = [pltpu.VMEM((rows, wide_own), F32), pltpu.VMEM((traps, wide_own), F32)] if crossing else []
    slm, weights = call(
        functools.partial(final_kernel, per_row, crossing),
        "final",
        [((2, per_row, modes), F32), ((traps, count), F32)],
        [VMEM] * (4 + len(extra)),
        out_specs=[any_space, any_space],
        scratch=[
            pltpu.VMEM((2, per_row, modes), F32),
            pltpu.VMEM((traps, count), F32),
            pltpu.SemaphoreType.DMA((1 + per_row // 16,)),
        ]
        + room,
        **cost,
    )(old, mine, away, back, *extra)

    return jnp.transpose(field, (1, 0, 2)), weights.T, jnp.transpose(slm, (2, 0, 1))


def solution(mesh):
    placed = (P(None, "row", "col"), P("col", "row"), P(), P(), P())
    return jax.shard_map(
        body,
        mesh=mesh,
        in_specs=placed,
        out_specs=(P(("row", "col"), None, None), P(), P("col", None, "row")),
        check_vma=False,
    )
```

```python
import functools

import jax
import jax.numpy as jnp
from jax import lax
from jax.experimental import pallas as pl
from jax.experimental.pallas import tpu as pltpu
from jax.sharding import PartitionSpec as P

MODES = 16384
TRAPS = 64
BF = jnp.bfloat16
F32 = jnp.float32
AXES = ("row", "col")
LANES = 128
SIN = (0.9999996052826214, -0.16666553769418907, 0.008332409691364227, -0.00019808794770261517, 2.6998844729663915e-06,
       -2.0368733379709898e-08)
COS = (0.999999989217114, -0.49999989221470714, 0.041666490704389186, -0.0013887810304225767, 2.4770020037729276e-05,
       -2.708030902998698e-07, 1.7249574387300172e-09)
STEEP = 25.0
CROSS = 6
NT = (((1,), (1,)), ((), ()))
NN = (((1,), (0,)), ((), ()))
VMEM = pl.BlockSpec(memory_space=pltpu.VMEM)


def call(kernel, name, outs, ins, out_specs=None, scratch=(), flops=0, size=0):
    return pl.pallas_call(
        kernel,
        out_shape=[jax.ShapeDtypeStruct(s, d) for s, d in outs],
        in_specs=ins,
        out_specs=out_specs or [VMEM] * len(outs),
        scratch_shapes=list(scratch),
        compiler_params=pltpu.CompilerParams(vmem_limit_bytes=40 * 1024 * 1024),
        cost_estimate=pl.CostEstimate(flops=flops, bytes_accessed=size, transcendentals=0),
        name=name,
    )


def bits_of(n):
    return n.bit_length() - 1


def padded(n):
    return -(-2 * n // LANES) * LANES


def horner(coefs, y):
    acc = jnp.full_like(y, coefs[-1])
    for c in coefs[-2::-1]:
        acc = acc * y + c
    return acc


def swap_pairs(x, mask):
    n = lax.axis_size("row") * lax.axis_size("col")
    return lax.ppermute(x, AXES, [(i, i ^ mask) for i in range(n)])


def lane_of(x):
    return lax.broadcasted_iota(jnp.int32, x.shape, x.ndim - 1)


def turn(x, by):
    lanes = x.shape[-1]
    by = by % lanes
    return x if by == 0 else pltpu.roll(x, lanes - by, x.ndim - 1)


def flip_blocks(x, width, bit):
    w = width << bit
    return jnp.where((lane_of(x) // w) % 2 == 1, turn(x, -w), turn(x, w))


def spread(x, base, n):
    parts = []
    for c in range(padded(n) // LANES):
        at = LANES * c
        first, second = turn(x, at + base), turn(x, at + base - n)
        parts.append(jnp.where(lane_of(x) + at < n, first, second))
    return parts[0] if len(parts) == 1 else jnp.concatenate(parts, axis=1)


def partner(x, n):
    return jnp.where(lane_of(x) < n, turn(x, n), turn(x, -n))


def tree_sum(parts):
    while len(parts) > 1:
        parts = [parts[i] + parts[i + 1] for i in range(0, len(parts), 2)]
    return parts[0]


def relative(x, row, per_row):
    for b in range(bits_of(x.shape[1] // per_row)):
        x = jnp.where(((row >> b) & 1) == 1, flip_blocks(x, per_row, b), x)
    return x


def project(phase, t_ref, index, out_ref):
    n = phase.shape[0]
    rows = t_ref.shape[1]
    traps, lanes = index.shape
    y = phase * phase
    co = horner(COS, y).astype(BF)
    si = (phase * horner(SIN, y)).astype(BF)
    fill = [jnp.zeros((lanes - 2 * n, phase.shape[1]), BF)] if lanes > 2 * n else []
    out_ref[...] = lax.dot_general(
        t_ref[0], jnp.concatenate([co, si] + fill, axis=0), NT, preferred_element_type=F32
    ) + lax.dot_general(t_ref[1], jnp.concatenate([-si, co] + fill, axis=0), NT, preferred_element_type=F32)
    found = []
    for g in range(traps // 8):
        high = index[g * 8:(g + 1) * 8] >> 3
        low = index[g * 8:(g + 1) * 8] & 7
        got = jnp.zeros((8, lanes), F32)
        for h in range(rows // 8):
            got = jnp.where(high == h, jnp.take_along_axis(out_ref[h * 8:(h + 1) * 8, :], low, axis=0), got)
        found.append(got)
    return found


def own_kernel(ph_ref, index_ref, t_ref, out_ref, trap_ref):
    per_row = ph_ref.shape[0]
    row = lax.axis_index("row")
    index = spread(relative(index_ref[...], row, per_row) - row * t_ref.shape[1], 0, per_row)
    for g, got in enumerate(project(ph_ref[...], t_ref, index, out_ref)):
        trap_ref[g * 8:(g + 1) * 8, :] = got


def other_kernel(order, per_row, code_ref, index_ref, t_ref, own_ref, own_trap_ref, trap_ref, keep_ref, send_ref, out_ref):
    row, col = lax.axis_index("row"), lax.axis_index("col")
    traps, count = index_ref.shape
    rows = t_ref.shape[1]
    index = spread(relative(index_ref[...], row, per_row) - row * rows, per_row, count - per_row)
    code = code_ref[...].astype(F32)
    size = jnp.log(jnp.abs(code)) * (1.0 / STEEP)
    found = project(jnp.where(code < 0, -size, size), t_ref, index, out_ref)
    n_own = own_ref.shape[1] // LANES
    sets = [(own_ref, c) for c in range(n_own)] + [(out_ref, c) for c in range(out_ref.shape[1] // LANES)]
    parts = len(sets)
    for g in range(traps // 8):
        for p, (ref, c) in enumerate(sets):
            lanes = slice(c * LANES, (c + 1) * LANES)
            at = p * traps + g * 8
            trap_ref[at:at + 8, :] = own_trap_ref[g * 8:(g + 1) * 8, lanes] if p < n_own else found[g][:, lanes]
    px = rows // len(order)
    half = len(order) // 2
    for s, j in enumerate(order):
        start = pl.multiple_of((col ^ j) * px, px)
        for p, (ref, c) in enumerate(sets):
            piece = ref[pl.ds(start, px), c * LANES:(c + 1) * LANES]
            at = ((s % half) * parts + p) * px
            if s < half:
                keep_ref[at:at + px, :] = piece
            else:
                send_ref[at:at + px, :] = piece.astype(BF)


def plan_kernel(per_row, rows, index_ref, levels_ref, old_ref, now_ref, *refs):
    row = lax.axis_index("row")
    count = index_ref.shape[1]
    target = relative(levels_ref[...], row, per_row).astype(F32)
    old = relative(old_ref[...], row, per_row)
    mine = relative(index_ref[...], row, per_row) - row * rows
    now_ref[...] = mine
    refs[0][...] = old
    theirs = mine + (2 * row - 1) * rows
    refs[-1][...] = theirs
    inverse = 1.0 / target
    numer = old * (target * target)
    for s, (base, n) in enumerate(((0, per_row), (per_row, count - per_row))):
        idx_ref, inv_ref, num_ref = refs[1 + 3 * s:4 + 3 * s]
        idx_ref[...] = spread(mine, base, n)
        inv_ref[...] = spread(inverse, base, n)
        num_ref[...] = spread(numer, base, n)


def slot_kernel(sets, now_ref, *slot_refs):
    traps, count = now_ref.shape
    group = 8

    def find(g, carry):
        start = pl.multiple_of(g * (8 * group), 8 * group)
        pixels = [lax.broadcasted_iota(jnp.int32, (8, count), 0) + (start + 8 * i) for i in range(group)]
        acc = [jnp.full((8, count), -1, jnp.int32) for _ in range(group)]
        for k in range(traps):
            ind = jnp.broadcast_to(now_ref[k:k + 1, :], (8, count))
            for i in range(group):
                acc[i] = jnp.where(ind == pixels[i], k, acc[i])
        for i in range(group):
            for ref, (base, n) in zip(slot_refs, sets):
                ref[pl.ds(start + 8 * i, 8), :] = spread(acc[i], base, n)
        return carry

    lax.fori_loop(0, slot_refs[0].shape[0] // (8 * group), find, 0)


def joined(idx_ref, value_ref):
    traps, lanes = idx_ref.shape
    index = idx_ref[...]
    acc = [jnp.zeros((8, lanes), F32) for _ in range(traps // 8)]
    for k in range(traps):
        ind = jnp.broadcast_to(idx_ref[k:k + 1, :], (8, lanes))
        val = jnp.broadcast_to(value_ref[k:k + 1, :], (8, lanes))
        for g in range(traps // 8):
            acc[g] += jnp.where(index[g * 8:(g + 1) * 8, :] == ind, val, 0.0)
    return acc


def scatter(acc, slot_ref, px_ref, n):
    lanes = slot_ref.shape[1]
    for h in range(slot_ref.shape[0] // 8):
        slot = slot_ref[h * 8:(h + 1) * 8, :]
        high = slot >> 3
        low = slot & 7
        got = jnp.zeros((8, lanes), F32)
        for g in range(len(acc)):
            got = jnp.where(high == g, jnp.take_along_axis(acc[g], low, axis=0), got)
        px_ref[h * 8:(h + 1) * 8, :] = got
    proj = px_ref[...].astype(BF).T
    turned = [proj[n:2 * n], -proj[:n]] + ([proj[2 * n:]] if lanes > 2 * n else [])
    return proj, jnp.concatenate(turned, axis=0)


def back_through(pair, t_ref, first, last):
    return lax.dot_general(pair[0], t_ref[0, :, first:last], NN, preferred_element_type=F32) + lax.dot_general(
        pair[1], t_ref[1, :, first:last], NN, preferred_element_type=F32
    )


def values_kernel(per_row, crossing, trap_ref, t_ref, *refs):
    sets = (refs[0:3], refs[3:6])
    slot_ref, value_own_ref, away_ref, value_oth_ref, px_ref = refs[6:]
    rows, modes = t_ref.shape[1:]
    traps = sets[0][0].shape[0]
    ratios = []
    part = 0
    for (idx_ref, inv_ref, num_ref), value_ref, n in zip(sets, (value_own_ref, value_oth_ref), (per_row, LANES - per_row)):
        chunks = []
        for c in range(idx_ref.shape[1] // LANES):
            at = slice(part * traps, (part + 1) * traps)
            chunks.append(trap_ref[at, :])
            part += 1
        v = chunks[0] if len(chunks) == 1 else jnp.concatenate(chunks, axis=1)
        within = (idx_ref[...] >= 0) & (idx_ref[...] < rows)
        square = v * v
        amp2 = square + partner(square, n) + 0.25
        ratios.append(jnp.where(within, jnp.sqrt(amp2) * inv_ref[...], 0.0))
        value_ref[...] = jnp.where(within, num_ref[...] / amp2 * v, 0.0)
    own_lanes = lane_of(ratios[0][:, :LANES]) < per_row
    q = jnp.where(own_lanes, ratios[0][:, :LANES], turn(ratios[1][:, :LANES], -per_row)).astype(BF)
    n = LANES - per_row
    acc = joined(sets[1][0], value_oth_ref)
    back = back_through(scatter(acc, slot_ref, px_ref, n), t_ref, crossing, modes)
    for j in range(n // per_row):
        away_ref[j, :traps, :] = q
        at = traps
        if crossing:
            away_ref[j, at:at + traps, :] = jnp.concatenate(acc, axis=0).astype(BF)
            at += traps
        for w in range((modes - crossing) // LANES):
            lanes = slice(w * LANES, (w + 1) * LANES)
            away_ref[j, at:at + per_row, :] = back[j * per_row:(j + 1) * per_row, lanes].astype(BF)
            at += per_row
            away_ref[j, at:at + per_row, :] = back[n + j * per_row:n + (j + 1) * per_row, lanes].astype(BF)
            at += per_row


def far_kernel(per_row, far_ref, field_ref):
    px = field_ref.shape[1]
    own = far_ref[:px, :]
    others = [far_ref[at:at + px, :] for at in range(px, far_ref.shape[0], px)]
    others = others[0] if len(others) == 1 else jnp.concatenate(others, axis=1)
    n = LANES - per_row
    first = lane_of(own) < per_row
    for part in range(2):
        theirs = turn(turn(others, part * n)[:, :LANES], -per_row)
        both = jnp.where(first, turn(own, part * per_row), theirs)
        field_ref[part] = relative(both, lax.axis_index("row"), per_row).astype(BF)


def mine_kernel(per_row, value_ref, idx_ref, slot_ref, t_ref, mine_ref, px_ref):
    pair = scatter(joined(idx_ref, value_ref), slot_ref, px_ref, per_row)
    mine_ref[...] = back_through(pair, t_ref, 0, t_ref.shape[2])[:2 * per_row]


def final_kernel(per_row, crossing, old_ref, mine_ref, sent_ref, got_ref, *refs):
    slm_ref, weights_ref, out_ref, scaled_ref, sems = refs[2:7] if crossing else refs
    traps, count = old_ref.shape
    n_rows = count // per_row
    modes = mine_ref.shape[1]
    q = [sent_ref[0, :traps, :].astype(F32)]
    for m in range(1, n_rows):
        x = got_ref[m - 1, :traps, :].astype(F32)
        for b in range(bits_of(n_rows)):
            if (m >> b) & 1:
                x = flip_blocks(x, per_row, b)
        q.append(x)
    q = tree_sum(q)
    mean = jnp.sum(q, axis=0, keepdims=True) / TRAPS
    copies = []
    scale = jnp.broadcast_to(mean, (count, count)).T[:per_row, 0:1]
    scale = scale * jnp.sqrt(jnp.float32(MODES) / jnp.float32(TRAPS))
    at = traps
    across = []
    if crossing:
        slot_ref, t_ref = refs[:2]
        acc = [got_ref[0, at + g * 8:at + (g + 1) * 8, :].astype(F32) for g in range(traps // 8)]
        at += traps
        across = [back_through(scatter(acc, slot_ref, refs[7], per_row), t_ref, 0, crossing)]
    step = 16
    for i in range(per_row // step):
        halves = []
        for part in range(2):
            first = part * per_row + i * step
            total = mine_ref[first:first + step, :]
            theirs = [x[first:first + step] for x in across]
            for w in range((modes - crossing) // LANES):
                piece = 0.0
                for m in range(n_rows - 1):
                    piece = piece + got_ref[m, at + 2 * w * per_row + first:at + 2 * w * per_row + first + step, :].astype(F32)
                theirs.append(piece)
            total = total + jnp.concatenate(theirs, axis=1)
            halves.append(total * scale[i * step:(i + 1) * step])
        inv = lax.rsqrt(halves[0] * halves[0] + halves[1] * halves[1] + 1.0)
        for part in range(2):
            out_ref[part, i * step:(i + 1) * step, :] = halves[part] * inv
        piece = pl.ds(i * step, step)
        copies.append(pltpu.make_async_copy(out_ref.at[:, piece, :], slm_ref.at[:, piece, :], sems.at[i + 1]))
        copies[-1].start()
        if i == 0:
            scaled_ref[...] = relative(old_ref[...] * mean / q, lax.axis_index("row"), per_row)
            copies.append(pltpu.make_async_copy(scaled_ref, weights_ref, sems.at[0]))
            copies[-1].start()
    for copy in copies:
        copy.wait()


def body(transfer, phase, trap_index, levels, weights_old):
    n_rows = lax.axis_size("row")
    n_cols = lax.axis_size("col")
    rows, modes = transfer.shape[1:]
    count, traps = trap_index.shape
    per_row = count // n_rows
    px = rows // n_cols
    steps = bits_of(n_cols)
    masks = [1] + [(1 << b) | 1 for b in range(1, steps)]
    order = []
    for s in range(n_cols):
        j = 0
        for k in range(steps):
            if (s >> (steps - 1 - k)) & 1:
                j ^= masks[k]
        order.append(j)
    wide_own, wide_oth = padded(per_row), padded(count - per_row)
    parts = (wide_own + wide_oth) // LANES
    crossing = modes * CROSS // 8 // LANES * LANES if n_rows == 2 else 0
    phase_t = phase.T
    code = jnp.where(phase_t < 0, -1.0, 1.0) * jnp.exp(STEEP * jnp.abs(phase_t))
    code = code.astype(BF)
    others = [swap_pairs(code, m * n_cols) for m in range(1, n_rows)]
    other = others[0] if n_rows == 2 else jnp.concatenate(others, axis=0)

    cost = dict(flops=1, size=1)
    index, target, old = trap_index.T, levels.T, weights_old.T
    any_space = pl.BlockSpec(memory_space=pl.ANY)
    sets = (wide_own, wide_oth)
    now, old, *tables, now_cross = call(
        functools.partial(plan_kernel, per_row, rows),
        "plan",
        [((traps, count), jnp.int32), ((traps, count), F32)]
        + [((traps, wide), d) for wide in sets for d in (jnp.int32, F32, F32)]
        + [((traps, count), jnp.int32)],
        [VMEM] * 3,
        **cost,
    )(index, target, old)

    if crossing:
        t_across = swap_pairs(transfer[:, :, :crossing], n_cols)
    other, now = lax.optimization_barrier((other, now))
    own_out, own_trap = call(
        own_kernel,
        "own",
        [((rows, wide_own), F32), ((traps, wide_own), F32)],
        [VMEM, VMEM, VMEM],
        **cost,
    )(phase_t, index, transfer)
    n_half = rows * parts // 2
    n_trap = parts * traps
    trap, keep, send = call(
        functools.partial(other_kernel, order, per_row),
        "other",
        [((n_trap, LANES), F32), ((n_half, LANES), F32), ((n_half, LANES), BF)],
        [VMEM] * 5,
        scratch=[pltpu.VMEM((rows, wide_oth), F32)],
        flops=3 * 10**10,
        size=1,
    )(other, index, transfer, own_out, own_trap)

    own_set, oth_set = (0, per_row), (per_row, count - per_row)

    def plan_slots(now, *which):
        return call(
            functools.partial(slot_kernel, which),
            "slots",
            [((rows, padded(n)), jnp.int32) for _, n in which],
            [VMEM],
            **cost,
        )(now)

    groups = [list(range(1, min(3, steps)))] + [[b] for b in range(3, steps)]

    def sums(trap, keep, send, now):
        block = keep + swap_pairs(send, masks[0]).astype(F32)
        trap = trap + swap_pairs(trap, masks[0])
        trap, now = lax.optimization_barrier((trap, now))
        slots = plan_slots(now, own_set, oth_set)
        for group in groups:
            short = trap.astype(BF)
            ways = 1 << len(group)
            part = block.shape[0] // ways
            whole = block
            fields, traps_of = [whole[:part]], [short]
            for way in range(1, ways):
                mask = 0
                for i, b in enumerate(group):
                    if (way >> (len(group) - 1 - i)) & 1:
                        mask ^= masks[b]
                load = jnp.concatenate([short, whole[way * part:(way + 1) * part].astype(BF)], axis=0)
                got = swap_pairs(load, mask)
                traps_of.append(got[:short.shape[0]])
                fields.append(got[short.shape[0]:])
            trap = tree_sum([x.astype(F32) for x in traps_of])
            block = tree_sum([x.astype(F32) for x in fields])
            if group[0] == 1:
                trap, *slots = lax.optimization_barrier((trap, *slots))
        return (trap, block, *slots)

    if crossing:
        shapes = jax.eval_shape(sums, trap, keep, send, now)
        trap, block, *slots = lax.cond(
            trap_index[0, 0] >= 0, sums, lambda *args: tuple(jnp.zeros(x.shape, x.dtype) for x in shapes), trap, keep, send, now
        )
    else:
        trap, block, *slots = sums(trap, keep, send, now)

    n_away = traps * (2 if crossing else 1) + 2 * per_row * (modes - crossing) // LANES
    value_own, away = call(
        functools.partial(values_kernel, per_row, crossing),
        "values",
        [((traps, wide_own), F32), ((n_rows - 1, n_away, LANES), BF)],
        [VMEM] * 9,
        scratch=[pltpu.VMEM((traps, wide_oth), F32), pltpu.VMEM((rows, wide_oth), F32)],
        **cost,
    )(trap, transfer, *tables, slots[1])
    back = [swap_pairs(away[m - 1], m * n_cols)[None] for m in range(1, n_rows)]
    back = back[0] if n_rows == 2 else jnp.concatenate(back, axis=0)
    (field,) = call(functools.partial(far_kernel, per_row), "far", [((2, px, count), BF)], [VMEM], **cost)(block)
    (mine,) = call(
        functools.partial(mine_kernel, per_row),
        "mine",
        [((2 * per_row, modes), F32)],
        [VMEM] * 4,
        scratch=[pltpu.VMEM((rows, wide_own), F32)],
        **cost,
    )(value_own, tables[0], slots[0], transfer)
    if crossing:
        mine, now_cross = lax.optimization_barrier((mine, now_cross))
        (slots_cross,) = plan_slots(now_cross, own_set)
    extra = [slots_cross, t_across] if crossing else []
    room = [pltpu.VMEM((rows, wide_own), F32)] if crossing else []
    slm, weights = call(
        functools.partial(final_kernel, per_row, crossing),
        "final",
        [((2, per_row, modes), F32), ((traps, count), F32)],
        [VMEM] * (4 + len(extra)),
        out_specs=[any_space, any_space],
        scratch=[
            pltpu.VMEM((2, per_row, modes), F32),
            pltpu.VMEM((traps, count), F32),
            pltpu.SemaphoreType.DMA((1 + per_row // 16,)),
        ]
        + room,
        **cost,
    )(old, mine, away, back, *extra)

    return jnp.transpose(field, (1, 0, 2)), weights.T, jnp.transpose(slm, (2, 0, 1))


def solution(mesh):
    placed = (P(None, "row", "col"), P("col", "row"), P(), P(), P())
    return jax.shard_map(
        body,
        mesh=mesh,
        in_specs=placed,
        out_specs=(P(("row", "col"), None, None), P(), P("col", None, "row")),
        check_vma=False,
    )
```

```python
import functools

import jax
import jax.numpy as jnp
from jax import lax
from jax.experimental import pallas as pl
from jax.experimental.pallas import tpu as pltpu
from jax.sharding import PartitionSpec as P

MODES = 16384
TRAPS = 64
BF = jnp.bfloat16
F32 = jnp.float32
AXES = ("row", "col")
LANES = 128
SIN = (0.9999996052826214, -0.16666553769418907, 0.008332409691364227, -0.00019808794770261517, 2.6998844729663915e-06,
       -2.0368733379709898e-08)
COS = (0.999999989217114, -0.49999989221470714, 0.041666490704389186, -0.0013887810304225767, 2.4770020037729276e-05,
       -2.708030902998698e-07, 1.7249574387300172e-09)
STEEP = 25.0
CROSS = 6
NT = (((1,), (1,)), ((), ()))
NN = (((1,), (0,)), ((), ()))
VMEM = pl.BlockSpec(memory_space=pltpu.VMEM)


def call(kernel, name, outs, ins, out_specs=None, scratch=(), flops=0, size=0):
    return pl.pallas_call(
        kernel,
        out_shape=[jax.ShapeDtypeStruct(s, d) for s, d in outs],
        in_specs=ins,
        out_specs=out_specs or [VMEM] * len(outs),
        scratch_shapes=list(scratch),
        compiler_params=pltpu.CompilerParams(vmem_limit_bytes=40 * 1024 * 1024),
        cost_estimate=pl.CostEstimate(flops=flops, bytes_accessed=size, transcendentals=0),
        name=name,
    )


def bits_of(n):
    return n.bit_length() - 1


def padded(n):
    return -(-2 * n // LANES) * LANES


def horner(coefs, y):
    acc = jnp.full_like(y, coefs[-1])
    for c in coefs[-2::-1]:
        acc = acc * y + c
    return acc


def swap_pairs(x, mask):
    n = lax.axis_size("row") * lax.axis_size("col")
    return lax.ppermute(x, AXES, [(i, i ^ mask) for i in range(n)])


def lane_of(x):
    return lax.broadcasted_iota(jnp.int32, x.shape, x.ndim - 1)


def turn(x, by):
    lanes = x.shape[-1]
    by = by % lanes
    return x if by == 0 else pltpu.roll(x, lanes - by, x.ndim - 1)


def flip_blocks(x, width, bit):
    w = width << bit
    return jnp.where((lane_of(x) // w) % 2 == 1, turn(x, -w), turn(x, w))


def spread(x, base, n):
    parts = []
    for c in range(padded(n) // LANES):
        at = LANES * c
        first, second = turn(x, at + base), turn(x, at + base - n)
        parts.append(jnp.where(lane_of(x) + at < n, first, second))
    return parts[0] if len(parts) == 1 else jnp.concatenate(parts, axis=1)


def partner(x, n):
    return jnp.where(lane_of(x) < n, turn(x, n), turn(x, -n))


def tree_sum(parts):
    while len(parts) > 1:
        parts = [parts[i] + parts[i + 1] for i in range(0, len(parts), 2)]
    return parts[0]


def relative(x, row, per_row):
    for b in range(bits_of(x.shape[1] // per_row)):
        x = jnp.where(((row >> b) & 1) == 1, flip_blocks(x, per_row, b), x)
    return x


def project(phase, t_ref, index, out_ref):
    n = phase.shape[0]
    rows = t_ref.shape[1]
    traps, lanes = index.shape
    y = phase * phase
    co = horner(COS, y).astype(BF)
    si = (phase * horner(SIN, y)).astype(BF)
    fill = [jnp.zeros((lanes - 2 * n, phase.shape[1]), BF)] if lanes > 2 * n else []
    out_ref[...] = lax.dot_general(
        t_ref[0], jnp.concatenate([co, si] + fill, axis=0), NT, preferred_element_type=F32
    ) + lax.dot_general(t_ref[1], jnp.concatenate([-si, co] + fill, axis=0), NT, preferred_element_type=F32)
    found = []
    for g in range(traps // 8):
        high = index[g * 8:(g + 1) * 8] >> 3
        low = index[g * 8:(g + 1) * 8] & 7
        got = jnp.zeros((8, lanes), F32)
        for h in range(rows // 8):
            got = jnp.where(high == h, jnp.take_along_axis(out_ref[h * 8:(h + 1) * 8, :], low, axis=0), got)
        found.append(got)
    return found


def own_kernel(ph_ref, index_ref, t_ref, out_ref, trap_ref):
    per_row = ph_ref.shape[0]
    row = lax.axis_index("row")
    index = spread(relative(index_ref[...], row, per_row) - row * t_ref.shape[1], 0, per_row)
    for g, got in enumerate(project(ph_ref[...], t_ref, index, out_ref)):
        trap_ref[g * 8:(g + 1) * 8, :] = got


def other_kernel(order, per_row, code_ref, index_ref, t_ref, own_ref, own_trap_ref, trap_ref, keep_ref, send_ref, out_ref):
    row, col = lax.axis_index("row"), lax.axis_index("col")
    traps, count = index_ref.shape
    rows = t_ref.shape[1]
    index = spread(relative(index_ref[...], row, per_row) - row * rows, per_row, count - per_row)
    code = code_ref[...].astype(F32)
    size = jnp.log(jnp.abs(code)) * (1.0 / STEEP)
    found = project(jnp.where(code < 0, -size, size), t_ref, index, out_ref)
    n_own = own_ref.shape[1] // LANES
    sets = [(own_ref, c) for c in range(n_own)] + [(out_ref, c) for c in range(out_ref.shape[1] // LANES)]
    parts = len(sets)
    for g in range(traps // 8):
        for p, (ref, c) in enumerate(sets):
            lanes = slice(c * LANES, (c + 1) * LANES)
            at = p * traps + g * 8
            trap_ref[at:at + 8, :] = own_trap_ref[g * 8:(g + 1) * 8, lanes] if p < n_own else found[g][:, lanes]
    px = rows // len(order)
    half = len(order) // 2
    for s, j in enumerate(order):
        start = pl.multiple_of((col ^ j) * px, px)
        for p, (ref, c) in enumerate(sets):
            piece = ref[pl.ds(start, px), c * LANES:(c + 1) * LANES]
            at = ((s % half) * parts + p) * px
            if s < half:
                keep_ref[at:at + px, :] = piece
            else:
                send_ref[at:at + px, :] = piece.astype(BF)


def plan_kernel(per_row, rows, index_ref, levels_ref, old_ref, now_ref, *refs):
    row = lax.axis_index("row")
    count = index_ref.shape[1]
    target = relative(levels_ref[...], row, per_row).astype(F32)
    old = relative(old_ref[...], row, per_row)
    mine = relative(index_ref[...], row, per_row) - row * rows
    now_ref[...] = mine
    refs[0][...] = old
    theirs = mine + (2 * row - 1) * rows
    refs[-1][...] = theirs
    inverse = 1.0 / target
    numer = old * (target * target)
    for s, (base, n) in enumerate(((0, per_row), (per_row, count - per_row))):
        idx_ref, inv_ref, num_ref = refs[1 + 3 * s:4 + 3 * s]
        idx_ref[...] = spread(mine, base, n)
        inv_ref[...] = spread(inverse, base, n)
        num_ref[...] = spread(numer, base, n)


def slot_kernel(sets, now_ref, *slot_refs):
    traps, count = now_ref.shape
    group = 8

    def find(g, carry):
        start = pl.multiple_of(g * (8 * group), 8 * group)
        pixels = [lax.broadcasted_iota(jnp.int32, (8, count), 0) + (start + 8 * i) for i in range(group)]
        acc = [jnp.full((8, count), -1, jnp.int32) for _ in range(group)]
        for k in range(traps):
            ind = jnp.broadcast_to(now_ref[k:k + 1, :], (8, count))
            for i in range(group):
                acc[i] = jnp.where(ind == pixels[i], k, acc[i])
        for i in range(group):
            for ref, (base, n) in zip(slot_refs, sets):
                ref[pl.ds(start + 8 * i, 8), :] = spread(acc[i], base, n)
        return carry

    lax.fori_loop(0, slot_refs[0].shape[0] // (8 * group), find, 0)


def joined(idx_ref, value_ref):
    traps, lanes = idx_ref.shape
    index = idx_ref[...]
    acc = [jnp.zeros((8, lanes), F32) for _ in range(traps // 8)]
    for k in range(traps):
        ind = jnp.broadcast_to(idx_ref[k:k + 1, :], (8, lanes))
        val = jnp.broadcast_to(value_ref[k:k + 1, :], (8, lanes))
        for g in range(traps // 8):
            acc[g] += jnp.where(index[g * 8:(g + 1) * 8, :] == ind, val, 0.0)
    return acc


def scatter(acc, slot_ref, px_ref, n):
    lanes = slot_ref.shape[1]
    for h in range(slot_ref.shape[0] // 8):
        slot = slot_ref[h * 8:(h + 1) * 8, :]
        high = slot >> 3
        low = slot & 7
        got = jnp.zeros((8, lanes), F32)
        for g in range(len(acc)):
            got = jnp.where(high == g, jnp.take_along_axis(acc[g], low, axis=0), got)
        px_ref[h * 8:(h + 1) * 8, :] = got
    proj = px_ref[...].astype(BF).T
    turned = [proj[n:2 * n], -proj[:n]] + ([proj[2 * n:]] if lanes > 2 * n else [])
    return proj, jnp.concatenate(turned, axis=0)


def back_through(pair, t_ref, first, last):
    return lax.dot_general(pair[0], t_ref[0, :, first:last], NN, preferred_element_type=F32) + lax.dot_general(
        pair[1], t_ref[1, :, first:last], NN, preferred_element_type=F32
    )


def values_kernel(per_row, crossing, trap_ref, t_ref, *refs):
    sets = (refs[0:3], refs[3:6])
    slot_ref, value_own_ref, away_ref, value_oth_ref, px_ref = refs[6:]
    rows, modes = t_ref.shape[1:]
    traps = sets[0][0].shape[0]
    ratios = []
    part = 0
    for (idx_ref, inv_ref, num_ref), value_ref, n in zip(sets, (value_own_ref, value_oth_ref), (per_row, LANES - per_row)):
        chunks = []
        for c in range(idx_ref.shape[1] // LANES):
            at = slice(part * traps, (part + 1) * traps)
            chunks.append(trap_ref[at, :])
            part += 1
        v = chunks[0] if len(chunks) == 1 else jnp.concatenate(chunks, axis=1)
        within = (idx_ref[...] >= 0) & (idx_ref[...] < rows)
        square = v * v
        amp2 = square + partner(square, n) + 0.25
        ratios.append(jnp.where(within, jnp.sqrt(amp2) * inv_ref[...], 0.0))
        value_ref[...] = jnp.where(within, num_ref[...] / amp2 * v, 0.0)
    own_lanes = lane_of(ratios[0][:, :LANES]) < per_row
    q = jnp.where(own_lanes, ratios[0][:, :LANES], turn(ratios[1][:, :LANES], -per_row)).astype(BF)
    n = LANES - per_row
    acc = joined(sets[1][0], value_oth_ref)
    back = back_through(scatter(acc, slot_ref, px_ref, n), t_ref, crossing, modes)
    for j in range(n // per_row):
        away_ref[j, :traps, :] = q
        at = traps
        if crossing:
            away_ref[j, at:at + traps, :] = jnp.concatenate(acc, axis=0).astype(BF)
            at += traps
        for w in range((modes - crossing) // LANES):
            lanes = slice(w * LANES, (w + 1) * LANES)
            away_ref[j, at:at + per_row, :] = back[j * per_row:(j + 1) * per_row, lanes].astype(BF)
            at += per_row
            away_ref[j, at:at + per_row, :] = back[n + j * per_row:n + (j + 1) * per_row, lanes].astype(BF)
            at += per_row


def far_kernel(per_row, far_ref, field_ref):
    px = field_ref.shape[1]
    own = far_ref[:px, :]
    others = [far_ref[at:at + px, :] for at in range(px, far_ref.shape[0], px)]
    others = others[0] if len(others) == 1 else jnp.concatenate(others, axis=1)
    n = LANES - per_row
    first = lane_of(own) < per_row
    for part in range(2):
        theirs = turn(turn(others, part * n)[:, :LANES], -per_row)
        both = jnp.where(first, turn(own, part * per_row), theirs)
        field_ref[part] = relative(both, lax.axis_index("row"), per_row).astype(BF)


def mine_kernel(per_row, value_ref, idx_ref, slot_ref, t_ref, mine_ref, px_ref):
    pair = scatter(joined(idx_ref, value_ref), slot_ref, px_ref, per_row)
    mine_ref[...] = back_through(pair, t_ref, 0, t_ref.shape[2])[:2 * per_row]


def final_kernel(per_row, crossing, old_ref, mine_ref, sent_ref, got_ref, *refs):
    slm_ref, weights_ref, out_ref, scaled_ref, sems = refs[2:7] if crossing else refs
    traps, count = old_ref.shape
    n_rows = count // per_row
    modes = mine_ref.shape[1]
    q = [sent_ref[0, :traps, :].astype(F32)]
    for m in range(1, n_rows):
        x = got_ref[m - 1, :traps, :].astype(F32)
        for b in range(bits_of(n_rows)):
            if (m >> b) & 1:
                x = flip_blocks(x, per_row, b)
        q.append(x)
    q = tree_sum(q)
    mean = jnp.sum(q, axis=0, keepdims=True) / TRAPS
    copies = []
    scale = jnp.broadcast_to(mean, (count, count)).T[:per_row, 0:1]
    scale = scale * jnp.sqrt(jnp.float32(MODES) / jnp.float32(TRAPS))
    at = traps
    across = []
    if crossing:
        slot_ref, t_ref = refs[:2]
        acc = [got_ref[0, at + g * 8:at + (g + 1) * 8, :].astype(F32) for g in range(traps // 8)]
        at += traps
        across = [back_through(scatter(acc, slot_ref, refs[7], per_row), t_ref, 0, crossing)]
    step = 16
    for i in range(per_row // step):
        halves = []
        for part in range(2):
            first = part * per_row + i * step
            total = mine_ref[first:first + step, :]
            theirs = [x[first:first + step] for x in across]
            for w in range((modes - crossing) // LANES):
                piece = 0.0
                for m in range(n_rows - 1):
                    piece = piece + got_ref[m, at + 2 * w * per_row + first:at + 2 * w * per_row + first + step, :].astype(F32)
                theirs.append(piece)
            total = total + jnp.concatenate(theirs, axis=1)
            halves.append(total * scale[i * step:(i + 1) * step])
        inv = lax.rsqrt(halves[0] * halves[0] + halves[1] * halves[1] + 1.0)
        for part in range(2):
            out_ref[part, i * step:(i + 1) * step, :] = halves[part] * inv
        piece = pl.ds(i * step, step)
        copies.append(pltpu.make_async_copy(out_ref.at[:, piece, :], slm_ref.at[:, piece, :], sems.at[i + 1]))
        copies[-1].start()
        if i == 0:
            scaled_ref[...] = relative(old_ref[...] * mean / q, lax.axis_index("row"), per_row)
            copies.append(pltpu.make_async_copy(scaled_ref, weights_ref, sems.at[0]))
            copies[-1].start()
    for copy in copies:
        copy.wait()


def body(transfer, phase, trap_index, levels, weights_old):
    n_rows = lax.axis_size("row")
    n_cols = lax.axis_size("col")
    rows, modes = transfer.shape[1:]
    count, traps = trap_index.shape
    per_row = count // n_rows
    px = rows // n_cols
    steps = bits_of(n_cols)
    masks = [1] + [(1 << b) | 1 for b in range(1, steps)]
    order = []
    for s in range(n_cols):
        j = 0
        for k in range(steps):
            if (s >> (steps - 1 - k)) & 1:
                j ^= masks[k]
        order.append(j)
    wide_own, wide_oth = padded(per_row), padded(count - per_row)
    parts = (wide_own + wide_oth) // LANES
    crossing = modes * CROSS // 8 // LANES * LANES if n_rows == 2 else 0
    phase_t = phase.T
    code = jnp.where(phase_t < 0, -1.0, 1.0) * jnp.exp(STEEP * jnp.abs(phase_t))
    code = code.astype(BF)
    others = [swap_pairs(code, m * n_cols) for m in range(1, n_rows)]
    other = others[0] if n_rows == 2 else jnp.concatenate(others, axis=0)

    cost = dict(flops=1, size=1)
    index, target, old = trap_index.T, levels.T, weights_old.T
    any_space = pl.BlockSpec(memory_space=pl.ANY)
    sets = (wide_own, wide_oth)
    now, old, *tables, now_cross = call(
        functools.partial(plan_kernel, per_row, rows),
        "plan",
        [((traps, count), jnp.int32), ((traps, count), F32)]
        + [((traps, wide), d) for wide in sets for d in (jnp.int32, F32, F32)]
        + [((traps, count), jnp.int32)],
        [VMEM] * 3,
        **cost,
    )(index, target, old)

    valid = trap_index[0, 0] >= 0
    if crossing:
        piece, now_cross, valid = lax.optimization_barrier((transfer[:, :, :crossing], now_cross, valid))
        t_across = swap_pairs(piece, n_cols)
    other, now = lax.optimization_barrier((other, now))
    own_out, own_trap = call(
        own_kernel,
        "own",
        [((rows, wide_own), F32), ((traps, wide_own), F32)],
        [VMEM, VMEM, VMEM],
        **cost,
    )(phase_t, index, transfer)
    n_half = rows * parts // 2
    n_trap = parts * traps
    trap, keep, send = call(
        functools.partial(other_kernel, order, per_row),
        "other",
        [((n_trap, LANES), F32), ((n_half, LANES), F32), ((n_half, LANES), BF)],
        [VMEM] * 5,
        scratch=[pltpu.VMEM((rows, wide_oth), F32)],
        flops=3 * 10**10,
        size=1,
    )(other, index, transfer, own_out, own_trap)

    own_set, oth_set = (0, per_row), (per_row, count - per_row)

    def plan_slots(now, *which):
        return call(
            functools.partial(slot_kernel, which),
            "slots",
            [((rows, padded(n)), jnp.int32) for _, n in which],
            [VMEM],
            **cost,
        )(now)

    groups = [list(range(1, min(3, steps)))] + [[b] for b in range(3, steps)]

    def sums(trap, keep, send, now):
        block = keep + swap_pairs(send, masks[0]).astype(F32)
        trap = trap + swap_pairs(trap, masks[0])
        trap, now = lax.optimization_barrier((trap, now))
        slots = plan_slots(now, own_set, oth_set)
        for group in groups:
            short = trap.astype(BF)
            ways = 1 << len(group)
            part = block.shape[0] // ways
            whole = block
            fields, traps_of = [whole[:part]], [short]
            for way in range(1, ways):
                mask = 0
                for i, b in enumerate(group):
                    if (way >> (len(group) - 1 - i)) & 1:
                        mask ^= masks[b]
                load = jnp.concatenate([short, whole[way * part:(way + 1) * part].astype(BF)], axis=0)
                got = swap_pairs(load, mask)
                traps_of.append(got[:short.shape[0]])
                fields.append(got[short.shape[0]:])
            trap = tree_sum([x.astype(F32) for x in traps_of])
            block = tree_sum([x.astype(F32) for x in fields])
            if group[0] == 1:
                trap, *slots = lax.optimization_barrier((trap, *slots))
        return (trap, block, *slots)

    if crossing:
        shapes = jax.eval_shape(sums, trap, keep, send, now)
        trap, block, *slots = lax.cond(
            valid, sums, lambda *args: tuple(jnp.zeros(x.shape, x.dtype) for x in shapes), trap, keep, send, now
        )
    else:
        trap, block, *slots = sums(trap, keep, send, now)

    n_away = traps * (2 if crossing else 1) + 2 * per_row * (modes - crossing) // LANES
    value_own, away = call(
        functools.partial(values_kernel, per_row, crossing),
        "values",
        [((traps, wide_own), F32), ((n_rows - 1, n_away, LANES), BF)],
        [VMEM] * 9,
        scratch=[pltpu.VMEM((traps, wide_oth), F32), pltpu.VMEM((rows, wide_oth), F32)],
        **cost,
    )(trap, transfer, *tables, slots[1])
    back = [swap_pairs(away[m - 1], m * n_cols)[None] for m in range(1, n_rows)]
    back = back[0] if n_rows == 2 else jnp.concatenate(back, axis=0)
    (field,) = call(functools.partial(far_kernel, per_row), "far", [((2, px, count), BF)], [VMEM], **cost)(block)
    (mine,) = call(
        functools.partial(mine_kernel, per_row),
        "mine",
        [((2 * per_row, modes), F32)],
        [VMEM] * 4,
        scratch=[pltpu.VMEM((rows, wide_own), F32)],
        **cost,
    )(value_own, tables[0], slots[0], transfer)
    if crossing:
        mine, now_cross = lax.optimization_barrier((mine, now_cross))
        (slots_cross,) = plan_slots(now_cross, own_set)
    extra = [slots_cross, t_across] if crossing else []
    room = [pltpu.VMEM((rows, wide_own), F32)] if crossing else []
    slm, weights = call(
        functools.partial(final_kernel, per_row, crossing),
        "final",
        [((2, per_row, modes), F32), ((traps, count), F32)],
        [VMEM] * (4 + len(extra)),
        out_specs=[any_space, any_space],
        scratch=[
            pltpu.VMEM((2, per_row, modes), F32),
            pltpu.VMEM((traps, count), F32),
            pltpu.SemaphoreType.DMA((1 + per_row // 16,)),
        ]
        + room,
        **cost,
    )(old, mine, away, back, *extra)

    return jnp.transpose(field, (1, 0, 2)), weights.T, jnp.transpose(slm, (2, 0, 1))


def solution(mesh):
    placed = (P(None, "row", "col"), P("col", "row"), P(), P(), P())
    return jax.shard_map(
        body,
        mesh=mesh,
        in_specs=placed,
        out_specs=(P(("row", "col"), None, None), P(), P("col", None, "row")),
        check_vma=False,
    )
```

```python
import functools

import jax
import jax.numpy as jnp
from jax import lax
from jax.experimental import pallas as pl
from jax.experimental.pallas import tpu as pltpu
from jax.sharding import PartitionSpec as P

MODES = 16384
TRAPS = 64
BF = jnp.bfloat16
F32 = jnp.float32
AXES = ("row", "col")
LANES = 128
SIN = (0.9999996052826214, -0.16666553769418907, 0.008332409691364227, -0.00019808794770261517, 2.6998844729663915e-06,
       -2.0368733379709898e-08)
COS = (0.999999989217114, -0.49999989221470714, 0.041666490704389186, -0.0013887810304225767, 2.4770020037729276e-05,
       -2.708030902998698e-07, 1.7249574387300172e-09)
STEEP = 25.0
CROSS = 6
NT = (((1,), (1,)), ((), ()))
NN = (((1,), (0,)), ((), ()))
VMEM = pl.BlockSpec(memory_space=pltpu.VMEM)


def call(kernel, name, outs, ins, out_specs=None, scratch=(), flops=0, size=0):
    return pl.pallas_call(
        kernel,
        out_shape=[jax.ShapeDtypeStruct(s, d) for s, d in outs],
        in_specs=ins,
        out_specs=out_specs or [VMEM] * len(outs),
        scratch_shapes=list(scratch),
        compiler_params=pltpu.CompilerParams(vmem_limit_bytes=40 * 1024 * 1024),
        cost_estimate=pl.CostEstimate(flops=flops, bytes_accessed=size, transcendentals=0),
        name=name,
    )


def bits_of(n):
    return n.bit_length() - 1


def padded(n):
    return -(-2 * n // LANES) * LANES


def horner(coefs, y):
    acc = jnp.full_like(y, coefs[-1])
    for c in coefs[-2::-1]:
        acc = acc * y + c
    return acc


def swap_pairs(x, mask):
    n = lax.axis_size("row") * lax.axis_size("col")
    return lax.ppermute(x, AXES, [(i, i ^ mask) for i in range(n)])


def lane_of(x):
    return lax.broadcasted_iota(jnp.int32, x.shape, x.ndim - 1)


def turn(x, by):
    lanes = x.shape[-1]
    by = by % lanes
    return x if by == 0 else pltpu.roll(x, lanes - by, x.ndim - 1)


def flip_blocks(x, width, bit):
    w = width << bit
    return jnp.where((lane_of(x) // w) % 2 == 1, turn(x, -w), turn(x, w))


def spread(x, base, n):
    parts = []
    for c in range(padded(n) // LANES):
        at = LANES * c
        first, second = turn(x, at + base), turn(x, at + base - n)
        parts.append(jnp.where(lane_of(x) + at < n, first, second))
    return parts[0] if len(parts) == 1 else jnp.concatenate(parts, axis=1)


def partner(x, n):
    return jnp.where(lane_of(x) < n, turn(x, n), turn(x, -n))


def tree_sum(parts):
    while len(parts) > 1:
        parts = [parts[i] + parts[i + 1] for i in range(0, len(parts), 2)]
    return parts[0]


def relative(x, row, per_row):
    for b in range(bits_of(x.shape[1] // per_row)):
        x = jnp.where(((row >> b) & 1) == 1, flip_blocks(x, per_row, b), x)
    return x


def project(phase, t_ref, index, out_ref):
    n = phase.shape[0]
    rows = t_ref.shape[1]
    traps, lanes = index.shape
    y = phase * phase
    co = horner(COS, y).astype(BF)
    si = (phase * horner(SIN, y)).astype(BF)
    fill = [jnp.zeros((lanes - 2 * n, phase.shape[1]), BF)] if lanes > 2 * n else []
    out_ref[...] = lax.dot_general(
        t_ref[0], jnp.concatenate([co, si] + fill, axis=0), NT, preferred_element_type=F32
    ) + lax.dot_general(t_ref[1], jnp.concatenate([-si, co] + fill, axis=0), NT, preferred_element_type=F32)
    found = []
    for g in range(traps // 8):
        high = index[g * 8:(g + 1) * 8] >> 3
        low = index[g * 8:(g + 1) * 8] & 7
        got = jnp.zeros((8, lanes), F32)
        for h in range(rows // 8):
            got = jnp.where(high == h, jnp.take_along_axis(out_ref[h * 8:(h + 1) * 8, :], low, axis=0), got)
        found.append(got)
    return found


def own_kernel(ph_ref, index_ref, t_ref, out_ref, trap_ref):
    per_row = ph_ref.shape[0]
    row = lax.axis_index("row")
    index = spread(relative(index_ref[...], row, per_row) - row * t_ref.shape[1], 0, per_row)
    for g, got in enumerate(project(ph_ref[...], t_ref, index, out_ref)):
        trap_ref[g * 8:(g + 1) * 8, :] = got


def other_kernel(order, per_row, code_ref, index_ref, t_ref, own_ref, own_trap_ref, trap_ref, keep_ref, send_ref, out_ref):
    row, col = lax.axis_index("row"), lax.axis_index("col")
    traps, count = index_ref.shape
    rows = t_ref.shape[1]
    index = spread(relative(index_ref[...], row, per_row) - row * rows, per_row, count - per_row)
    code = code_ref[...].astype(F32)
    size = jnp.log(jnp.abs(code)) * (1.0 / STEEP)
    found = project(jnp.where(code < 0, -size, size), t_ref, index, out_ref)
    n_own = own_ref.shape[1] // LANES
    sets = [(own_ref, c) for c in range(n_own)] + [(out_ref, c) for c in range(out_ref.shape[1] // LANES)]
    parts = len(sets)
    for g in range(traps // 8):
        for p, (ref, c) in enumerate(sets):
            lanes = slice(c * LANES, (c + 1) * LANES)
            at = p * traps + g * 8
            trap_ref[at:at + 8, :] = own_trap_ref[g * 8:(g + 1) * 8, lanes] if p < n_own else found[g][:, lanes]
    px = rows // len(order)
    half = len(order) // 2
    for s, j in enumerate(order):
        start = pl.multiple_of((col ^ j) * px, px)
        for p, (ref, c) in enumerate(sets):
            piece = ref[pl.ds(start, px), c * LANES:(c + 1) * LANES]
            at = ((s % half) * parts + p) * px
            if s < half:
                keep_ref[at:at + px, :] = piece
            else:
                send_ref[at:at + px, :] = piece.astype(BF)


def plan_kernel(per_row, rows, index_ref, levels_ref, old_ref, now_ref, *refs):
    row = lax.axis_index("row")
    count = index_ref.shape[1]
    target = relative(levels_ref[...], row, per_row).astype(F32)
    old = relative(old_ref[...], row, per_row)
    mine = relative(index_ref[...], row, per_row) - row * rows
    now_ref[...] = mine
    refs[0][...] = old
    theirs = mine + (2 * row - 1) * rows
    refs[-1][...] = theirs
    inverse = 1.0 / target
    numer = old * (target * target)
    for s, (base, n) in enumerate(((0, per_row), (per_row, count - per_row))):
        idx_ref, inv_ref, num_ref = refs[1 + 3 * s:4 + 3 * s]
        idx_ref[...] = spread(mine, base, n)
        inv_ref[...] = spread(inverse, base, n)
        num_ref[...] = spread(numer, base, n)


def slot_kernel(sets, now_ref, *slot_refs):
    traps, count = now_ref.shape
    group = 8

    def find(g, carry):
        start = pl.multiple_of(g * (8 * group), 8 * group)
        pixels = [lax.broadcasted_iota(jnp.int32, (8, count), 0) + (start + 8 * i) for i in range(group)]
        acc = [jnp.full((8, count), -1, jnp.int32) for _ in range(group)]
        for k in range(traps):
            ind = jnp.broadcast_to(now_ref[k:k + 1, :], (8, count))
            for i in range(group):
                acc[i] = jnp.where(ind == pixels[i], k, acc[i])
        for i in range(group):
            for ref, (base, n) in zip(slot_refs, sets):
                ref[pl.ds(start + 8 * i, 8), :] = spread(acc[i], base, n)
        return carry

    lax.fori_loop(0, slot_refs[0].shape[0] // (8 * group), find, 0)


def joined(idx_ref, value_ref):
    traps, lanes = idx_ref.shape
    index = idx_ref[...]
    acc = [jnp.zeros((8, lanes), F32) for _ in range(traps // 8)]
    for k in range(traps):
        ind = jnp.broadcast_to(idx_ref[k:k + 1, :], (8, lanes))
        val = jnp.broadcast_to(value_ref[k:k + 1, :], (8, lanes))
        for g in range(traps // 8):
            acc[g] += jnp.where(index[g * 8:(g + 1) * 8, :] == ind, val, 0.0)
    return acc


def scatter(acc, slot_ref, px_ref, n):
    lanes = slot_ref.shape[1]
    for h in range(slot_ref.shape[0] // 8):
        slot = slot_ref[h * 8:(h + 1) * 8, :]
        high = slot >> 3
        low = slot & 7
        got = jnp.zeros((8, lanes), F32)
        for g in range(len(acc)):
            got = jnp.where(high == g, jnp.take_along_axis(acc[g], low, axis=0), got)
        px_ref[h * 8:(h + 1) * 8, :] = got
    proj = px_ref[...].astype(BF).T
    turned = [proj[n:2 * n], -proj[:n]] + ([proj[2 * n:]] if lanes > 2 * n else [])
    return proj, jnp.concatenate(turned, axis=0)


def back_through(pair, t_ref, first, last):
    return lax.dot_general(pair[0], t_ref[0, :, first:last], NN, preferred_element_type=F32) + lax.dot_general(
        pair[1], t_ref[1, :, first:last], NN, preferred_element_type=F32
    )


def values_kernel(per_row, crossing, trap_ref, t_ref, *refs):
    sets = (refs[0:3], refs[3:6])
    slot_ref, value_own_ref, away_ref, value_oth_ref, px_ref = refs[6:]
    rows, modes = t_ref.shape[1:]
    traps = sets[0][0].shape[0]
    ratios = []
    part = 0
    for (idx_ref, inv_ref, num_ref), value_ref, n in zip(sets, (value_own_ref, value_oth_ref), (per_row, LANES - per_row)):
        chunks = []
        for c in range(idx_ref.shape[1] // LANES):
            at = slice(part * traps, (part + 1) * traps)
            chunks.append(trap_ref[at, :])
            part += 1
        v = chunks[0] if len(chunks) == 1 else jnp.concatenate(chunks, axis=1)
        within = (idx_ref[...] >= 0) & (idx_ref[...] < rows)
        square = v * v
        amp2 = square + partner(square, n) + 0.25
        ratios.append(jnp.where(within, jnp.sqrt(amp2) * inv_ref[...], 0.0))
        value_ref[...] = jnp.where(within, num_ref[...] / amp2 * v, 0.0)
    own_lanes = lane_of(ratios[0][:, :LANES]) < per_row
    q = jnp.where(own_lanes, ratios[0][:, :LANES], turn(ratios[1][:, :LANES], -per_row)).astype(BF)
    n = LANES - per_row
    acc = joined(sets[1][0], value_oth_ref)
    back = back_through(scatter(acc, slot_ref, px_ref, n), t_ref, crossing, modes)
    for j in range(n // per_row):
        away_ref[j, :traps, :] = q
        at = traps
        if crossing:
            away_ref[j, at:at + traps, :] = jnp.concatenate(acc, axis=0).astype(BF)
            at += traps
        for w in range((modes - crossing) // LANES):
            lanes = slice(w * LANES, (w + 1) * LANES)
            away_ref[j, at:at + per_row, :] = back[j * per_row:(j + 1) * per_row, lanes].astype(BF)
            at += per_row
            away_ref[j, at:at + per_row, :] = back[n + j * per_row:n + (j + 1) * per_row, lanes].astype(BF)
            at += per_row


def far_kernel(per_row, far_ref, field_ref):
    px = field_ref.shape[1]
    own = far_ref[:px, :]
    others = [far_ref[at:at + px, :] for at in range(px, far_ref.shape[0], px)]
    others = others[0] if len(others) == 1 else jnp.concatenate(others, axis=1)
    n = LANES - per_row
    first = lane_of(own) < per_row
    for part in range(2):
        theirs = turn(turn(others, part * n)[:, :LANES], -per_row)
        both = jnp.where(first, turn(own, part * per_row), theirs)
        field_ref[part] = relative(both, lax.axis_index("row"), per_row).astype(BF)


def mine_kernel(per_row, value_ref, idx_ref, slot_ref, t_ref, mine_ref, px_ref):
    pair = scatter(joined(idx_ref, value_ref), slot_ref, px_ref, per_row)
    mine_ref[...] = back_through(pair, t_ref, 0, t_ref.shape[2])[:2 * per_row]


def final_kernel(per_row, crossing, old_ref, mine_ref, sent_ref, got_ref, *refs):
    slm_ref, weights_ref, out_ref, scaled_ref, sems = refs[2:7] if crossing else refs
    traps, count = old_ref.shape
    n_rows = count // per_row
    modes = mine_ref.shape[1]
    q = [sent_ref[0, :traps, :].astype(F32)]
    for m in range(1, n_rows):
        x = got_ref[m - 1, :traps, :].astype(F32)
        for b in range(bits_of(n_rows)):
            if (m >> b) & 1:
                x = flip_blocks(x, per_row, b)
        q.append(x)
    q = tree_sum(q)
    mean = jnp.sum(q, axis=0, keepdims=True) / TRAPS
    copies = []
    scale = jnp.broadcast_to(mean, (count, count)).T[:per_row, 0:1]
    scale = scale * jnp.sqrt(jnp.float32(MODES) / jnp.float32(TRAPS))
    at = traps
    across = []
    if crossing:
        slot_ref, t_ref = refs[:2]
        acc = [got_ref[0, at + g * 8:at + (g + 1) * 8, :].astype(F32) for g in range(traps // 8)]
        at += traps
        across = [back_through(scatter(acc, slot_ref, refs[7], per_row), t_ref, 0, crossing)]
    step = 16
    for i in range(per_row // step):
        halves = []
        for part in range(2):
            first = part * per_row + i * step
            total = mine_ref[first:first + step, :]
            theirs = [x[first:first + step] for x in across]
            for w in range((modes - crossing) // LANES):
                piece = 0.0
                for m in range(n_rows - 1):
                    piece = piece + got_ref[m, at + 2 * w * per_row + first:at + 2 * w * per_row + first + step, :].astype(F32)
                theirs.append(piece)
            total = total + jnp.concatenate(theirs, axis=1)
            halves.append(total * scale[i * step:(i + 1) * step])
        inv = lax.rsqrt(halves[0] * halves[0] + halves[1] * halves[1] + 1.0)
        for part in range(2):
            out_ref[part, i * step:(i + 1) * step, :] = halves[part] * inv
        piece = pl.ds(i * step, step)
        copies.append(pltpu.make_async_copy(out_ref.at[:, piece, :], slm_ref.at[:, piece, :], sems.at[i + 1]))
        copies[-1].start()
        if i == 0:
            scaled_ref[...] = relative(old_ref[...] * mean / q, lax.axis_index("row"), per_row)
            copies.append(pltpu.make_async_copy(scaled_ref, weights_ref, sems.at[0]))
            copies[-1].start()
    for copy in copies:
        copy.wait()


def body(transfer, phase, trap_index, levels, weights_old):
    n_rows = lax.axis_size("row")
    n_cols = lax.axis_size("col")
    rows, modes = transfer.shape[1:]
    count, traps = trap_index.shape
    per_row = count // n_rows
    px = rows // n_cols
    steps = bits_of(n_cols)
    masks = [1] + [(1 << b) | 1 for b in range(1, steps)]
    order = []
    for s in range(n_cols):
        j = 0
        for k in range(steps):
            if (s >> (steps - 1 - k)) & 1:
                j ^= masks[k]
        order.append(j)
    wide_own, wide_oth = padded(per_row), padded(count - per_row)
    parts = (wide_own + wide_oth) // LANES
    crossing = modes * CROSS // 8 // LANES * LANES if n_rows == 2 else 0
    phase_t = phase.T
    code = jnp.where(phase_t < 0, -1.0, 1.0) * jnp.exp(STEEP * jnp.abs(phase_t))
    code = code.astype(BF)
    others = [swap_pairs(code, m * n_cols) for m in range(1, n_rows)]
    other = others[0] if n_rows == 2 else jnp.concatenate(others, axis=0)

    cost = dict(flops=1, size=1)
    index, target, old = trap_index.T, levels.T, weights_old.T
    any_space = pl.BlockSpec(memory_space=pl.ANY)
    sets = (wide_own, wide_oth)
    now, old, *tables, now_cross = call(
        functools.partial(plan_kernel, per_row, rows),
        "plan",
        [((traps, count), jnp.int32), ((traps, count), F32)]
        + [((traps, wide), d) for wide in sets for d in (jnp.int32, F32, F32)]
        + [((traps, count), jnp.int32)],
        [VMEM] * 3,
        **cost,
    )(index, target, old)

    valid = trap_index[0, 0] >= 0
    if crossing:
        piece, now_cross, valid = lax.optimization_barrier((transfer[:, :, :crossing], now_cross, valid))
        t_across = swap_pairs(piece, n_cols)
    other, now = lax.optimization_barrier((other, now))
    own_out, own_trap = call(
        own_kernel,
        "own",
        [((rows, wide_own), F32), ((traps, wide_own), F32)],
        [VMEM, VMEM, VMEM],
        **cost,
    )(phase_t, index, transfer)
    n_half = rows * parts // 2
    n_trap = parts * traps
    trap, keep, send = call(
        functools.partial(other_kernel, order, per_row),
        "other",
        [((n_trap, LANES), F32), ((n_half, LANES), F32), ((n_half, LANES), BF)],
        [VMEM] * 5,
        scratch=[pltpu.VMEM((rows, wide_oth), F32)],
        flops=3 * 10**10,
        size=1,
    )(other, index, transfer, own_out, own_trap)

    own_set, oth_set = (0, per_row), (per_row, count - per_row)

    def plan_slots(now, *which):
        return call(
            functools.partial(slot_kernel, which),
            "slots",
            [((rows, padded(n)), jnp.int32) for _, n in which],
            [VMEM],
            **cost,
        )(now)

    groups = [list(range(1, min(3, steps)))] + [[b] for b in range(3, steps)]

    def sums(trap, keep, send, now):
        block = keep + swap_pairs(send, masks[0]).astype(F32)
        trap = trap + swap_pairs(trap, masks[0])
        trap, now = lax.optimization_barrier((trap, now))
        slots = plan_slots(now, own_set, oth_set)
        for group in groups:
            short = trap.astype(BF)
            ways = 1 << len(group)
            part = block.shape[0] // ways
            whole = block
            fields, traps_of = [whole[:part]], [short]
            for way in range(1, ways):
                mask = 0
                for i, b in enumerate(group):
                    if (way >> (len(group) - 1 - i)) & 1:
                        mask ^= masks[b]
                away = whole[way * part:(way + 1) * part].astype(BF)
                if mask & 1:
                    got = swap_pairs(jnp.concatenate([short, away], axis=0), mask)
                    traps_of.append(got[:short.shape[0]])
                    fields.append(got[short.shape[0]:])
                else:
                    traps_of.append(swap_pairs(short, mask | 1))
                    fields.append(swap_pairs(away, mask))
            trap = tree_sum([x.astype(F32) for x in traps_of])
            block = tree_sum([x.astype(F32) for x in fields])
            if group[0] == 1:
                trap, *slots = lax.optimization_barrier((trap, *slots))
        return (trap, block, *slots)

    if crossing:
        shapes = jax.eval_shape(sums, trap, keep, send, now)
        trap, block, *slots = lax.cond(
            valid, sums, lambda *args: tuple(jnp.zeros(x.shape, x.dtype) for x in shapes), trap, keep, send, now
        )
    else:
        trap, block, *slots = sums(trap, keep, send, now)

    n_away = traps * (2 if crossing else 1) + 2 * per_row * (modes - crossing) // LANES
    value_own, away = call(
        functools.partial(values_kernel, per_row, crossing),
        "values",
        [((traps, wide_own), F32), ((n_rows - 1, n_away, LANES), BF)],
        [VMEM] * 9,
        scratch=[pltpu.VMEM((traps, wide_oth), F32), pltpu.VMEM((rows, wide_oth), F32)],
        **cost,
    )(trap, transfer, *tables, slots[1])
    back = [swap_pairs(away[m - 1], m * n_cols)[None] for m in range(1, n_rows)]
    back = back[0] if n_rows == 2 else jnp.concatenate(back, axis=0)
    (field,) = call(functools.partial(far_kernel, per_row), "far", [((2, px, count), BF)], [VMEM], **cost)(block)
    (mine,) = call(
        functools.partial(mine_kernel, per_row),
        "mine",
        [((2 * per_row, modes), F32)],
        [VMEM] * 4,
        scratch=[pltpu.VMEM((rows, wide_own), F32)],
        **cost,
    )(value_own, tables[0], slots[0], transfer)
    if crossing:
        mine, now_cross = lax.optimization_barrier((mine, now_cross))
        (slots_cross,) = plan_slots(now_cross, own_set)
    extra = [slots_cross, t_across] if crossing else []
    room = [pltpu.VMEM((rows, wide_own), F32)] if crossing else []
    slm, weights = call(
        functools.partial(final_kernel, per_row, crossing),
        "final",
        [((2, per_row, modes), F32), ((traps, count), F32)],
        [VMEM] * (4 + len(extra)),
        out_specs=[any_space, any_space],
        scratch=[
            pltpu.VMEM((2, per_row, modes), F32),
            pltpu.VMEM((traps, count), F32),
            pltpu.SemaphoreType.DMA((1 + per_row // 16,)),
        ]
        + room,
        **cost,
    )(old, mine, away, back, *extra)

    return jnp.transpose(field, (1, 0, 2)), weights.T, jnp.transpose(slm, (2, 0, 1))


def solution(mesh):
    placed = (P(None, "row", "col"), P("col", "row"), P(), P(), P())
    return jax.shard_map(
        body,
        mesh=mesh,
        in_specs=placed,
        out_specs=(P(("row", "col"), None, None), P(), P("col", None, "row")),
        check_vma=False,
    )
```
